1024 devices in a mesh: dom: 128 (over x, y, core), inst: 8 (over z).
Axes of the slice: x: 8, y: 8, z: 8, core: 2. Of those that a mesh axis runs over, the one named last changes fastest.
Arguments:
- adjoint: float32 [16, 5, 131072], P('inst', None, 'dom'), may hold values from -6 to 6
- gradient: float32 [16, 5, 131072], P('inst', None, 'dom'), may hold values from -6 to 6
- jac_blocks: float32 [16, 6, 5, 5, 131072], P('inst', None, None, None, 'dom'), may hold values from -0.9 to 0.9
- diag_inverse: float32 [16, 5, 5, 131072], P('inst', None, None, 'dom'), may hold values from -2.4 to 2.4
- volume: float32 [131072], P('dom'), may hold values from 0.05 to 0.2
- columns: int32 [6, 131072], P(None, 'dom'), may hold values from 0 to 1535, as said below
- send_rows: int32 [512, 128], P('dom'), may hold values from 0 to 1023, as said below
- counts: int32 [128], P('dom'), may hold values from 512 to 1024, as said below
Outputs:
- swept: float32 [16, 5, 131072], P('inst', None, 'dom')
The draws below stay inside these ranges and needn't reach their ends.
Inputs may be any that keep to these rules, and one draw needn't show every extreme that they name: `counts`: at least half of 1024 for every partition; some partition uses all 1024 slots. `columns`: for block k < 4 the entry is a live cell of the same partition; for the other two it is 1024 plus a row of the four interface blocks; every interface row of a partition is named by some live cell. `send_rows`: live cells of the sending partition.
All inputs are finite; a program needn't handle non-finite values.
Results may differ from the reference program's by a relative error of at most 0.0001.
Values sent between devices are 32-bit elements; how exact they have to be, the bound alone decides.
No kernel may reach another device: no remote copies, remote signals or barrier semaphores. Data moves between devices by JAX's collectives and lax.ppermute only.
A program may use at most 128 MiB of HBM per device.

```python
import math
import jax
import jax.numpy as jnp
from jax import lax

NI = 16
NV = 5
NBR = 6
IF = 128
CELLS = 1024
SWEEPS = 2
DOMAINS = 128
TOTAL = 131072


def cell_counts(key):
    key = jax.random.fold_in(key, 11)
    key_one, key_two = jax.random.split(key)
    drawn = jax.random.randint(key_one, (DOMAINS,), CELLS // 2, CELLS + 1)
    fullest = jax.random.randint(key_two, (), 0, DOMAINS)
    return jnp.where(jnp.arange(DOMAINS) == fullest, CELLS, drawn).astype(jnp.int32)


def draw_counts(key, part):
    return cell_counts(key)


def draw_columns(key, part):
    used = cell_counts(key)
    key = jax.random.fold_in(key, 2)
    key_one, key_two = jax.random.split(key)
    local_cols = jax.random.randint(key_one, (NBR - 2, DOMAINS, CELLS), 0, used[None, :, None])
    cover = CELLS + jnp.mod(jnp.arange(CELLS, dtype=jnp.int32), 4 * IF)
    cover_cols = jnp.broadcast_to(cover[None, None, :], (1, DOMAINS, CELLS))
    random_halo = CELLS + jax.random.randint(key_two, (1, DOMAINS, CELLS), 0, 4 * IF)
    stacked = jnp.concatenate([local_cols, cover_cols, random_halo], axis=0)
    return stacked.reshape(NBR, DOMAINS * CELLS).astype(jnp.int32)


def draw_send_rows(key, part):
    used = cell_counts(key)
    key = jax.random.fold_in(key, 3)
    picked = jax.random.randint(key, (DOMAINS, 4, IF), 0, used[:, None, None])
    fullest = jnp.argmax((used == CELLS).astype(jnp.int32))
    picked = picked.at[fullest, 0, 0].set(CELLS - 1)
    picked = picked.at[fullest, 0, 1].set(0)
    return picked.reshape(DOMAINS * 4, IF).astype(jnp.int32)


def block_scale(key, dims, cuts, low, largest):
    factor_of = 1.0
    for dim, parts in cuts:
        heights = jax.random.uniform(jax.random.fold_in(jax.random.fold_in(key, 6), dim), (parts,), jnp.float32, low / len(cuts), largest / len(cuts))
        factor_of = factor_of * jnp.repeat(jnp.exp(heights), dims[dim] // parts).reshape((-1,) + (1,) * (len(dims) - 1 - dim))
    return factor_of


def gaussian(own_key, shape, deviation, most, shards=(), kind=jnp.bfloat16):
    values = jax.random.normal(own_key, shape, jnp.float32) * deviation
    if len(shards) > 0:
        values = block_scale(own_key, shape, shards, -0.22, 0.18) * values
    return jnp.clip(values, min=-most, max=most).astype(kind)


def setup_inputs(seed: int = 0) -> dict:
    arg_keys = jax.random.split(jax.random.key(seed), 9)
    adjoint = gaussian(arg_keys[0], (NI, NV, TOTAL), 1.0, 6.0, ((0, 8), (2, 128)), jnp.float32)
    gradient = gaussian(arg_keys[1], (NI, NV, TOTAL), 1.0, 6.0, ((0, 8), (2, 128)), jnp.float32)
    jac_blocks = gaussian(arg_keys[2], (NI, NBR, NV, NV, TOTAL), 0.15, 0.9, ((0, 8), (4, 128)), jnp.float32)
    diag_inverse = gaussian(arg_keys[3], (NI, NV, NV, TOTAL), 0.4, 2.4, ((0, 8), (3, 128)), jnp.float32)
    volume = jnp.clip(jnp.exp(math.log(0.2) - 1.3862944 * jax.random.uniform(arg_keys[4], (TOTAL,), jnp.float32) ** block_scale(arg_keys[4], (TOTAL,), ((0, 128),), -0.2, 0.2)), 0.05, 0.2)
    columns = draw_columns(jax.random.fold_in(arg_keys[8], 71), 0)
    send_rows = draw_send_rows(jax.random.fold_in(arg_keys[8], 71), 0)
    counts = draw_counts(jax.random.fold_in(arg_keys[8], 71), 0)
    return {"adjoint": adjoint, "gradient": gradient, "jac_blocks": jac_blocks, "diag_inverse": diag_inverse, "volume": volume, "columns": columns, "send_rows": send_rows, "counts": counts}


OFFSETS = (1, -1, 2, -2)


def spectral_matrix():
    index = jnp.arange(NI, dtype=jnp.int32)
    differ = index[:, None] - index[None, :]
    parity = (1 - 2 * jnp.mod(differ, 2)).astype(jnp.float32)
    safe_diff = jnp.where(differ == 0, 1, differ).astype(jnp.float32)
    angle = math.pi * safe_diff / NI
    values = 0.5 * parity * jnp.cos(angle) / jnp.sin(angle)
    return jnp.where(differ == 0, 0.0, values).astype(jnp.float32)


def reference(adjoint, gradient, jac_blocks, diag_inverse, volume, columns, send_rows, counts):
    spectral = spectral_matrix()
    current = adjoint.reshape(NI, NV, DOMAINS, CELLS)
    grad_parts = gradient.reshape(NI, NV, DOMAINS, CELLS)
    blocks = jac_blocks.reshape(NI, NBR, NV, NV, DOMAINS, CELLS)
    inverse = diag_inverse.reshape(NI, NV, NV, DOMAINS, CELLS)
    vol_parts = volume.reshape(DOMAINS, CELLS)
    col_parts = columns.reshape(NBR, DOMAINS, CELLS)
    sends = send_rows.reshape(DOMAINS, 4, IF)
    live_mask = (jnp.arange(CELLS, dtype=jnp.int32)[None, :] < counts[:, None]).astype(jnp.float32)
    width = CELLS + 4 * IF
    col_wide = jnp.broadcast_to(col_parts[None], (NV, NBR, DOMAINS, CELLS))
    for sweep_index in range(SWEEPS):
        pieces = [current]
        for slot_index, offset in enumerate(OFFSETS):
            source_rows = jnp.roll(sends[:, slot_index, :], offset, axis=0)
            source_vals = jnp.roll(current, offset, axis=2)
            picked = jnp.take_along_axis(source_vals, jnp.broadcast_to(source_rows[None, None], (NI, NV, DOMAINS, IF)), axis=3)
            pieces.append(picked)
        extended = jnp.concatenate(pieces, axis=3)

        def couple(operands):
            blk, ext_one = operands
            wide = jnp.broadcast_to(ext_one[:, None], (NV, NBR, DOMAINS, width))
            gathered = jnp.take_along_axis(wide, col_wide, axis=3)
            return jnp.einsum('kijpc,jkpc->ipc', blk, gathered, precision=lax.Precision.HIGHEST)

        coupling = lax.map(couple, (blocks, extended))
        timewise = vol_parts[None, None] * jnp.einsum('mn,mvpc->nvpc', spectral, current, precision=lax.Precision.HIGHEST)
        remainder = grad_parts - coupling - timewise
        current = live_mask[None, None] * jnp.einsum('nijpc,njpc->nipc', inverse, remainder, precision=lax.Precision.HIGHEST)
    return current.reshape(NI, NV, TOTAL)
```

```python
import functools
import math

import jax
import jax.numpy as jnp
from jax import lax
from jax.experimental import pallas as pl
from jax.experimental.pallas import tpu as pltpu
from jax.sharding import PartitionSpec as P

NI = 16
NV = 5
NBR = 6
NEAR = 4
SLOTS = 4
OFFSETS = (1, -1, 2, -2)
LANES = 128
ROWS = 16
HALF = 8
BLOCKS = 8


def spectral(diff):
    diff = diff % NI
    if diff == 0:
        return 0.0
    angle = math.pi * diff / NI
    return 0.5 * (-1) ** diff * math.cos(angle) / math.sin(angle)


def dense(x):
    lead = x.shape[1:-1]
    n = len(lead)
    y = x.reshape((2,) + lead + (BLOCKS, LANES))
    y = y.transpose(tuple(range(1, n + 1)) + (n + 1, 0, n + 2))
    return y.reshape(lead + (ROWS, LANES))


def undense(y):
    lead = y.shape[:-2]
    n = len(lead)
    y = y.reshape(lead + (BLOCKS, 2, LANES))
    y = y.transpose((n + 1,) + tuple(range(n)) + (n, n + 2))
    return y.reshape((2,) + lead + (BLOCKS * LANES,))


def row_iota():
    return lax.broadcasted_iota(jnp.int32, (HALF, LANES), 0)


def pick_lanes(x, index):
    return jnp.take_along_axis(x, index, axis=1, mode="promise_in_bounds")


def pick_rows(x, index):
    return jnp.take_along_axis(x, index, axis=0, mode="promise_in_bounds")


def fill_table(half, value, var, table):
    parity = row_iota() & 1
    for q in range(4):
        table[var, 4 * half + q] = pick_rows(value, parity + 2 * q)


def pick(table, var, lane, masks):
    got = pick_lanes(table[var, 0], lane)
    for block in range(1, len(masks)):
        got = jnp.where(masks[block], pick_lanes(table[var, block], lane), got)
    return got


def split(index, blocks):
    high = lax.shift_right_logical(index, 7)
    return index & (LANES - 1), [high == block for block in range(blocks)]


def send_blocks(table, sends, rows, outs):
    for slot in range(SLOTS):
        rows[2 * slot : 2 * slot + 2, :] = jnp.broadcast_to(sends[slot : slot + 1, :], (2, LANES))
    lane, masks = split(rows[...], BLOCKS)
    parity = row_iota() & 1
    for var in range(NV):
        got = pick(table, var, lane, masks)
        for slot in range(SLOTS):
            outs[slot][var] = pick_rows(got, parity + 2 * slot)


def prep_kernel(adj, sends, out0, out1, out2, out3, copies, table, rows):
    for var in range(NV):
        for half in range(2):
            value = adj[var, half * HALF : (half + 1) * HALF, :]
            fill_table(half, value, var, table)
            for peer in range(8):
                at = var * ROWS + half * HALF
                copies[peer, at : at + HALF, :] = value
    send_blocks(table, sends, rows, (out0, out1, out2, out3))


def sweep_kernel(last, *refs):
    count, cur, every, h0, h1, h2, h3, jac, dinv, grad, vol, cols = refs[:12]
    halos = (h0, h1, h2, h3)
    if last:
        out, table, wide = refs[12:]
    else:
        sends, out, out0, out1, out2, out3, copies, table, wide, rows = refs[12:]
    me = lax.axis_index("inst")
    row = row_iota()
    parity = row & 1
    odd = parity == 1
    for var in range(NV):
        for half in range(2):
            fill_table(half, cur[var, half * HALF : (half + 1) * HALF, :], var, table)
    for k in range(NBR):
        for block in range(BLOCKS):
            one = cols[k : k + 1, block * LANES : (block + 1) * LANES]
            wide[k, 2 * block : 2 * block + 2, :] = jnp.broadcast_to(one, (2, LANES))
    fresh = []
    for half in range(2):
        here = slice(half * HALF, (half + 1) * HALF)
        coupling = [jnp.zeros((HALF, LANES), jnp.float32) for _ in range(NV)]
        for k in range(NBR):
            index = wide[k, here, :]
            if k < NEAR:
                lane, masks = split(index, BLOCKS)
            else:
                lane, masks = split(index - BLOCKS * LANES, SLOTS)
            for var in range(NV):
                if k < NEAR:
                    got = pick(table, var, lane, masks)
                else:
                    got = pick_lanes(halos[0][var], lane)
                    for slot in range(1, SLOTS):
                        got = jnp.where(masks[slot], pick_lanes(halos[slot][var], lane), got)
                for i in range(NV):
                    coupling[i] = coupling[i] + jac[k, i, var, here, :] * got
        volume = pick_rows(vol[...], lax.shift_right_logical(row, 1) + 4 * half)
        rest = []
        for var in range(NV):
            same = jnp.zeros((HALF, LANES), jnp.float32)
            cross = jnp.zeros((HALF, LANES), jnp.float32)
            for r in range(8):
                other = lax.rem(me + r, 8)
                at = var * ROWS + half * HALF
                value = every[other, at : at + HALF, :]
                if r:
                    same = same + spectral(2 * r) * value
                factor = jnp.where(odd, spectral(2 * r + 1), spectral(2 * r - 1))
                cross = cross + factor.astype(jnp.float32) * value
            timewise = same + pick_rows(cross, row ^ 1)
            rest.append(grad[var, here, :] - coupling[var] - volume * timewise)
        cell = (4 * half + lax.shift_right_logical(row, 1)) * LANES
        cell = cell + lax.broadcasted_iota(jnp.int32, (HALF, LANES), 1)
        live = (cell < count[0]).astype(jnp.float32)
        for i in range(NV):
            total = dinv[i, 0, here, :] * rest[0]
            for var in range(1, NV):
                total = total + dinv[i, var, here, :] * rest[var]
            total = live * total
            out[i, here, :] = total
            if not last:
                fresh.append((half, total, i))
                at = i * ROWS + half * HALF
                for peer in range(8):
                    copies[peer, at : at + HALF, :] = total
    if not last:
        for half, total, i in fresh:
            fill_table(half, total, i, table)
        send_blocks(table, sends, rows, (out0, out1, out2, out3))


VMEM = pl.BlockSpec(memory_space=pltpu.VMEM)
SMEM = pl.BlockSpec(memory_space=pltpu.SMEM)
PARAMS = pltpu.CompilerParams(vmem_limit_bytes=8 * 1024 * 1024)
TABLE = pltpu.VMEM((NV, BLOCKS, HALF, LANES), jnp.float32)
WIDE = pltpu.VMEM((NBR, ROWS, LANES), jnp.int32)
SENT = jax.ShapeDtypeStruct((NV, HALF, LANES), jnp.float32)
CURRENT = jax.ShapeDtypeStruct((NV, ROWS, LANES), jnp.float32)
COPIES = jax.ShapeDtypeStruct((8, NV * ROWS, LANES), jnp.float32)
ROW_INDEX = pltpu.VMEM((HALF, LANES), jnp.int32)


def exchange(blocks, copies):
    arrived = []
    for block, offset in zip(blocks, OFFSETS):
        count = lax.axis_size("dom")
        pairs = [(source, (source + offset) % count) for source in range(count)]
        arrived.append(lax.ppermute(block, "dom", pairs))
    return arrived, lax.all_to_all(copies, "inst", 0, 0)


def on_device(adjoint, gradient, jac_blocks, diag_inverse, volume, columns, send_rows, counts):
    cur, grad, jac, dinv = dense(adjoint), dense(gradient), dense(jac_blocks), dense(diag_inverse)
    vol = volume.reshape(BLOCKS, LANES)
    *blocks, copies = pl.pallas_call(
        prep_kernel,
        out_shape=(SENT,) * SLOTS + (COPIES,),
        in_specs=[VMEM] * 2,
        out_specs=(VMEM,) * 5,
        scratch_shapes=[TABLE, ROW_INDEX],
        compiler_params=PARAMS,
        name="prep",
    )(cur, send_rows)
    arrived, every = exchange(blocks, copies)
    cur, *blocks, copies = pl.pallas_call(
        functools.partial(sweep_kernel, False),
        out_shape=(CURRENT,) + (SENT,) * SLOTS + (COPIES,),
        in_specs=[SMEM] + [VMEM] * 12,
        out_specs=(VMEM,) * 6,
        scratch_shapes=[TABLE, WIDE, ROW_INDEX],
        compiler_params=PARAMS,
        name="sweep_one",
    )(counts, cur, every, *arrived, jac, dinv, grad, vol, columns, send_rows)
    arrived, every = exchange(blocks, copies)
    cur = pl.pallas_call(
        functools.partial(sweep_kernel, True),
        out_shape=CURRENT,
        in_specs=[SMEM] + [VMEM] * 11,
        out_specs=VMEM,
        scratch_shapes=[TABLE, WIDE],
        compiler_params=PARAMS,
        name="sweep_two",
    )(counts, cur, every, *arrived, jac, dinv, grad, vol, columns)
    return undense(cur)


def solution(mesh):
    in_specs = (
        P("inst", None, "dom"),
        P("inst", None, "dom"),
        P("inst", None, None, None, "dom"),
        P("inst", None, None, "dom"),
        P("dom"),
        P(None, "dom"),
        P("dom", None),
        P("dom"),
    )
    out_specs = P("inst", None, "dom")
    return jax.shard_map(
        on_device, mesh=mesh, in_specs=in_specs, out_specs=out_specs, check_vma=False
    )
```

```python
import functools
import math

import jax
import jax.numpy as jnp
from jax import lax
from jax.experimental import pallas as pl
from jax.experimental.pallas import tpu as pltpu
from jax.sharding import PartitionSpec as P

NI = 16
NV = 5
NBR = 6
NEAR = 4
SLOTS = 4
LANES = 128
ROWS = 16
HALF = 8
BLOCKS = 8


def spectral(diff):
    diff = diff % NI
    if diff == 0:
        return 0.0
    angle = math.pi * diff / NI
    return 0.5 * (-1) ** diff * math.cos(angle) / math.sin(angle)


def dense(x):
    lead = x.shape[1:-1]
    n = len(lead)
    y = x.reshape((2,) + lead + (BLOCKS, LANES))
    y = y.transpose(tuple(range(1, n + 1)) + (n + 1, 0, n + 2))
    return y.reshape(lead + (ROWS, LANES))


def undense(y):
    lead = y.shape[:-2]
    n = len(lead)
    y = y.reshape(lead + (BLOCKS, 2, LANES))
    y = y.transpose((n + 1,) + tuple(range(n)) + (n, n + 2))
    return y.reshape((2,) + lead + (BLOCKS * LANES,))


def row_iota():
    return lax.broadcasted_iota(jnp.int32, (HALF, LANES), 0)


def pick_lanes(x, index):
    return jnp.take_along_axis(x, index, axis=1, mode="promise_in_bounds")


def pick_rows(x, index):
    return jnp.take_along_axis(x, index, axis=0, mode="promise_in_bounds")


def fill_table(half, value, var, table):
    parity = row_iota() & 1
    for q in range(4):
        table[var, 4 * half + q] = pick_rows(value, parity + 2 * q)


def pick(table, var, lane, masks):
    got = pick_lanes(table[var, 0], lane)
    for block in range(1, len(masks)):
        got = jnp.where(masks[block], pick_lanes(table[var, block], lane), got)
    return got


def split(index, blocks):
    high = lax.shift_right_logical(index, 7)
    return index & (LANES - 1), [high == block for block in range(blocks)]


def send_blocks(table, rows, swap, own):
    lane, masks = split(rows, BLOCKS)
    parity = row_iota() & 1
    for var in range(NV):
        got = pick(table, var, lane, masks)
        for slot in range(SLOTS):
            out = (swap, swap, own, own)[slot]
            out[slot % 2, var] = pick_rows(got, parity + 2 * slot)


def prep_kernel(adj_hbm, sends_hbm, swap, own, copies, table, rows, adj, sends, sems):
    loads = [
        pltpu.make_async_copy(adj_hbm, adj, sems.at[0]),
        pltpu.make_async_copy(sends_hbm, sends, sems.at[1]),
    ]
    for load in loads:
        load.start()
    for load in loads:
        load.wait()
    for var in range(NV):
        for half in range(2):
            value = adj[var, half * HALF : (half + 1) * HALF, :]
            fill_table(half, value, var, table)
            for peer in range(8):
                at = var * ROWS + half * HALF
                copies[peer, at : at + HALF, :] = value
    for slot in range(SLOTS):
        rows[2 * slot : 2 * slot + 2, :] = jnp.broadcast_to(sends[slot : slot + 1, :], (2, LANES))
    send_blocks(table, rows[...], swap, own)


def pass_on(own, came, plus, minus):
    for var in range(NV):
        plus[0, var] = own[0, var]
        plus[1, var] = came[0, var]
        minus[0, var] = own[1, var]
        minus[1, var] = came[1, var]


def near_picks(table, wide, picked):
    for half in range(2):
        here = slice(half * HALF, (half + 1) * HALF)
        for k in range(NEAR):
            lane, masks = split(wide[k, here, :], BLOCKS)
            for var in range(NV):
                picked[k, var, here, :] = pick(table, var, lane, masks)


def near_sum(jac, picked, near):
    for half in range(2):
        here = slice(half * HALF, (half + 1) * HALF)
        total = [None] * NV
        for k in range(NEAR):
            for var in range(NV):
                got = picked[k, var, here, :]
                for i in range(NV):
                    term = jac[k, i, var, here, :] * got
                    total[i] = term if total[i] is None else total[i] + term
        for i in range(NV):
            near[i, here, :] = total[i]


def near_first(
    table, came, own, cols_hbm, jac_hbm, dinv_hbm, grad_hbm, vol_hbm, count,
    plus, minus, near, wide, jac, dinv, grad, volume, live,
    picked, cols, vol, sems,
):
    pairs = (
        (cols_hbm, cols),
        (jac_hbm, jac),
        (vol_hbm, vol),
        (dinv_hbm, dinv),
        (grad_hbm, grad),
    )
    loads = [pltpu.make_async_copy(a, b, sems.at[n]) for n, (a, b) in enumerate(pairs)]
    for load in loads:
        load.start()
    pass_on(own, came, plus, minus)
    loads[0].wait()
    for k in range(NBR):
        for block in range(BLOCKS):
            one = cols[k : k + 1, block * LANES : (block + 1) * LANES]
            wide[k, 2 * block : 2 * block + 2, :] = jnp.broadcast_to(one, (2, LANES))
    near_picks(table, wide, picked)
    for load in loads[1:]:
        load.wait()
    row = row_iota()
    for half in range(2):
        here = slice(half * HALF, (half + 1) * HALF)
        block = lax.shift_right_logical(row, 1) + 4 * half
        volume[here, :] = pick_rows(vol[...], block)
        cell = block * LANES + lax.broadcasted_iota(jnp.int32, (HALF, LANES), 1)
        live[here, :] = (cell < count[0]).astype(jnp.float32)
    near_sum(jac, picked, near)


def near_second(table, came, own, wide, jac, plus, minus, near, picked):
    pass_on(own, came, plus, minus)
    near_picks(table, wide, picked)
    near_sum(jac, picked, near)


def finish_kernel(last, *refs):
    every, came, above, below, near, wide, jac, dinv, grad, volume, live = refs[:11]
    if last:
        out, halos = refs[11:]
    else:
        rows, swap, own, copies, table, halos = refs[11:]
    me = lax.axis_index("inst")
    first = (lax.axis_index("dom") & 1) == 0
    row = row_iota()
    odd = (row & 1) == 1
    for var in range(NV):
        halos[0, var] = jnp.where(first, above[1, var], came[0, var])
        halos[1, var] = jnp.where(first, came[1, var], below[1, var])
        halos[2, var] = above[0, var]
        halos[3, var] = below[0, var]
    for half in range(2):
        here = slice(half * HALF, (half + 1) * HALF)
        coupling = [near[i, here, :] for i in range(NV)]
        for k in range(NEAR, NBR):
            lane, masks = split(wide[k, here, :] - BLOCKS * LANES, SLOTS)
            for var in range(NV):
                got = pick_lanes(halos[0, var], lane)
                for slot in range(1, SLOTS):
                    got = jnp.where(masks[slot], pick_lanes(halos[slot, var], lane), got)
                for i in range(NV):
                    coupling[i] = coupling[i] + jac[k, i, var, here, :] * got
        rest = []
        for var in range(NV):
            same = jnp.zeros((HALF, LANES), jnp.float32)
            cross = jnp.zeros((HALF, LANES), jnp.float32)
            for r in range(8):
                other = lax.rem(me + r, 8)
                at = var * ROWS + half * HALF
                value = every[other, at : at + HALF, :]
                if r:
                    same = same + spectral(2 * r) * value
                factor = jnp.where(odd, spectral(2 * r + 1), spectral(2 * r - 1))
                cross = cross + factor.astype(jnp.float32) * value
            timewise = same + pick_rows(cross, row ^ 1)
            rest.append(grad[var, here, :] - coupling[var] - volume[here, :] * timewise)
        for i in range(NV):
            total = dinv[i, 0, here, :] * rest[0]
            for var in range(1, NV):
                total = total + dinv[i, var, here, :] * rest[var]
            total = live[here, :] * total
            if last:
                out[i, here, :] = total
            else:
                fill_table(half, total, i, table)
                at = i * ROWS + half * HALF
                for peer in range(8):
                    copies[peer, at : at + HALF, :] = total
    if not last:
        send_blocks(table, rows[...], swap, own)


VMEM = pl.BlockSpec(memory_space=pltpu.VMEM)
HBM = pl.BlockSpec(memory_space=pltpu.HBM)
SMEM = pl.BlockSpec(memory_space=pltpu.SMEM)
PARAMS = pltpu.CompilerParams(vmem_limit_bytes=8 * 1024 * 1024)


def f32(*shape):
    return jax.ShapeDtypeStruct(shape, jnp.float32)


def i32(*shape):
    return jax.ShapeDtypeStruct(shape, jnp.int32)


TABLE = f32(NV, BLOCKS, HALF, LANES)
PAIR = f32(2, NV, HALF, LANES)
CURRENT = f32(NV, ROWS, LANES)
COPIES = f32(8, NV * ROWS, LANES)
WIDE = i32(NBR, ROWS, LANES)
ROW_INDEX = i32(HALF, LANES)
JAC = f32(NBR, NV, NV, ROWS, LANES)
DINV = f32(NV, NV, ROWS, LANES)
CELL = f32(ROWS, LANES)
PICKED = pltpu.VMEM((NEAR, NV, ROWS, LANES), jnp.float32)
HALOS = pltpu.VMEM((SLOTS, NV, HALF, LANES), jnp.float32)


def call(kernel, name, args, outs, scratch, hbm=(), smem=()):
    specs = [HBM if n in hbm else SMEM if n in smem else VMEM for n in range(len(args))]
    args = [
        pltpu.with_memory_space_constraint(arg, pltpu.HBM) if n in hbm else arg
        for n, arg in enumerate(args)
    ]
    return pl.pallas_call(
        kernel,
        out_shape=outs,
        in_specs=specs,
        out_specs=jax.tree.map(lambda _: VMEM, outs),
        scratch_shapes=scratch,
        compiler_params=PARAMS,
        name=name,
    )(*args)


def swapped(value):
    count = lax.axis_size("dom")
    return lax.ppermute(value, "dom", [(source, source ^ 1) for source in range(count)])


def shifted(value, steps):
    count = lax.axis_size("dom")
    pairs = [(source, (source + steps) % count) for source in range(count)]
    return lax.ppermute(value, "dom", pairs)


def on_device(adjoint, gradient, jac_blocks, diag_inverse, volume, columns, send_rows, counts):
    swap, own, copies, table, rows = call(
        prep_kernel,
        "prep",
        (dense(adjoint), send_rows),
        (PAIR, PAIR, COPIES, TABLE, ROW_INDEX),
        [
            pltpu.VMEM(CURRENT.shape, jnp.float32),
            pltpu.VMEM((SLOTS, LANES), jnp.int32),
            pltpu.SemaphoreType.DMA((2,)),
        ],
        hbm=(0, 1),
    )
    came = swapped(swap)
    every = lax.all_to_all(copies, "inst", 0, 0)
    raw = (
        columns,
        dense(jac_blocks),
        dense(diag_inverse),
        dense(gradient),
        volume.reshape(BLOCKS, LANES),
        counts,
    )
    plus, minus, near, wide, jac, dinv, grad, vol, live = call(
        near_first,
        "near_first",
        (table, came, own) + raw,
        (PAIR, PAIR, CURRENT, WIDE, JAC, DINV, CURRENT, CELL, CELL),
        [
            PICKED,
            pltpu.VMEM((NBR, BLOCKS * LANES), jnp.int32),
            pltpu.VMEM((BLOCKS, LANES), jnp.float32),
            pltpu.SemaphoreType.DMA((5,)),
        ],
        hbm=range(3, 8),
        smem=(8,),
    )
    kept = (wide, jac, dinv, grad, vol, live)
    swap, own, copies, table = call(
        functools.partial(finish_kernel, False),
        "finish_first",
        (every, came, shifted(plus, 2), shifted(minus, -2), near) + kept + (rows,),
        (PAIR, PAIR, COPIES, TABLE),
        [HALOS],
    )
    came = swapped(swap)
    every = lax.all_to_all(copies, "inst", 0, 0)
    plus, minus, near = call(
        near_second,
        "near_second",
        (table, came, own, wide, jac),
        (PAIR, PAIR, CURRENT),
        [PICKED],
    )
    out = call(
        functools.partial(finish_kernel, True),
        "finish_second",
        (every, came, shifted(plus, 2), shifted(minus, -2), near) + kept,
        CURRENT,
        [HALOS],
    )
    return undense(out)


def solution(mesh):
    in_specs = (
        P("inst", None, "dom"),
        P("inst", None, "dom"),
        P("inst", None, None, None, "dom"),
        P("inst", None, None, "dom"),
        P("dom"),
        P(None, "dom"),
        P("dom", None),
        P("dom"),
    )
    out_specs = P("inst", None, "dom")
    return jax.shard_map(
        on_device, mesh=mesh, in_specs=in_specs, out_specs=out_specs, check_vma=False
    )
```

```python
import functools
import math

import jax
import jax.numpy as jnp
from jax import lax
from jax.experimental import pallas as pl
from jax.experimental.pallas import tpu as pltpu
from jax.sharding import PartitionSpec as P

NI = 16
NV = 5
NBR = 6
NEAR = 4
SLOTS = 4
LANES = 128
ROWS = 16
HALF = 8
BLOCKS = 8


def spectral(diff):
    diff = diff % NI
    if diff == 0:
        return 0.0
    angle = math.pi * diff / NI
    return 0.5 * (-1) ** diff * math.cos(angle) / math.sin(angle)


def dense(x):
    lead = x.shape[1:-1]
    n = len(lead)
    y = x.reshape((2,) + lead + (BLOCKS, LANES))
    y = y.transpose(tuple(range(1, n + 1)) + (n + 1, 0, n + 2))
    return y.reshape(lead + (ROWS, LANES))


def undense(y):
    lead = y.shape[:-2]
    n = len(lead)
    y = y.reshape(lead + (BLOCKS, 2, LANES))
    y = y.transpose((n + 1,) + tuple(range(n)) + (n, n + 2))
    return y.reshape((2,) + lead + (BLOCKS * LANES,))


def row_iota():
    return lax.broadcasted_iota(jnp.int32, (HALF, LANES), 0)


def pick_lanes(x, index):
    return jnp.take_along_axis(x, index, axis=1, mode="promise_in_bounds")


def pick_rows(x, index):
    return jnp.take_along_axis(x, index, axis=0, mode="promise_in_bounds")


def fill_table(half, value, var, table):
    parity = row_iota() & 1
    for q in range(4):
        table[var, 4 * half + q] = pick_rows(value, parity + 2 * q)


def pick(table, var, lane, masks):
    got = pick_lanes(table[var, 0], lane)
    for block in range(1, len(masks)):
        got = jnp.where(masks[block], pick_lanes(table[var, block], lane), got)
    return got


def split(index, blocks):
    high = lax.shift_right_logical(index, 7)
    return index & (LANES - 1), [high == block for block in range(blocks)]


def send_blocks(table, rows, swap, own):
    lane, masks = split(rows, BLOCKS)
    parity = row_iota() & 1
    for var in range(NV):
        got = pick(table, var, lane, masks)
        for slot in range(SLOTS):
            out = (swap, swap, own, own)[slot]
            out[slot % 2, var] = pick_rows(got, parity + 2 * slot)


def prep_kernel(adj_hbm, sends_hbm, swap, own, copies, table, rows, adj, sends, sems):
    loads = [
        pltpu.make_async_copy(adj_hbm, adj, sems.at[0]),
        pltpu.make_async_copy(sends_hbm, sends, sems.at[1]),
    ]
    for load in loads:
        load.start()
    for load in loads:
        load.wait()
    for var in range(NV):
        for half in range(2):
            value = adj[var, half * HALF : (half + 1) * HALF, :]
            fill_table(half, value, var, table)
            for peer in range(8):
                at = var * ROWS + half * HALF
                copies[peer, at : at + HALF, :] = value
    for slot in range(SLOTS):
        rows[2 * slot : 2 * slot + 2, :] = jnp.broadcast_to(sends[slot : slot + 1, :], (2, LANES))
    send_blocks(table, rows[...], swap, own)


def join_kernel(own, came, plus, minus):
    for var in range(NV):
        plus[0, var] = own[0, var]
        plus[1, var] = came[0, var]
        minus[0, var] = own[1, var]
        minus[1, var] = came[1, var]


def timewise(every, me, var, half):
    row = row_iota()
    odd = (row & 1) == 1
    at = var * ROWS + half * HALF
    same = jnp.zeros((HALF, LANES), jnp.float32)
    cross = jnp.zeros((HALF, LANES), jnp.float32)
    for r in range(8):
        value = every[lax.rem(me + r, 8), at : at + HALF, :]
        if r:
            same = same + spectral(2 * r) * value
        factor = jnp.where(odd, spectral(2 * r + 1), spectral(2 * r - 1))
        cross = cross + factor.astype(jnp.float32) * value
    return same + pick_rows(cross, row ^ 1)


def inner(table, every, wide, jac, picked, grad, volume, rest, loads):
    me = lax.axis_index("inst")
    for half in range(2):
        here = slice(half * HALF, (half + 1) * HALF)
        for k in range(NEAR):
            lane, masks = split(wide[k, here, :], BLOCKS)
            for var in range(NV):
                picked[k, var, here, :] = pick(table, var, lane, masks)
        for var in range(NV):
            rest[var, here, :] = timewise(every, me, var, half)
    for load in loads:
        load.wait()
    for half in range(2):
        here = slice(half * HALF, (half + 1) * HALF)
        total = [None] * NV
        for k in range(NEAR):
            for var in range(NV):
                got = picked[k, var, here, :]
                for i in range(NV):
                    term = jac[k, i, var, here, :] * got
                    total[i] = term if total[i] is None else total[i] + term
        for i in range(NV):
            rest[i, here, :] = grad[i, here, :] - total[i] - volume(half) * rest[i, here, :]


def inner_first(
    table, every, cols_hbm, jac_hbm, dinv_hbm, grad_hbm, vol_hbm, count,
    rest, wide, jac, dinv, grad, volume, live,
    picked, cols, vol, sems,
):
    pairs = (
        (cols_hbm, cols),
        (jac_hbm, jac),
        (vol_hbm, vol),
        (dinv_hbm, dinv),
        (grad_hbm, grad),
    )
    loads = [pltpu.make_async_copy(a, b, sems.at[n]) for n, (a, b) in enumerate(pairs)]
    for load in loads:
        load.start()
    row = row_iota()
    for half in range(2):
        cell = (lax.shift_right_logical(row, 1) + 4 * half) * LANES
        cell = cell + lax.broadcasted_iota(jnp.int32, (HALF, LANES), 1)
        live[half * HALF : (half + 1) * HALF, :] = (cell < count[0]).astype(jnp.float32)
    loads[0].wait()
    for k in range(NBR):
        for block in range(BLOCKS):
            one = cols[k : k + 1, block * LANES : (block + 1) * LANES]
            wide[k, 2 * block : 2 * block + 2, :] = jnp.broadcast_to(one, (2, LANES))

    def spread(half):
        value = pick_rows(vol[...], lax.shift_right_logical(row, 1) + 4 * half)
        volume[half * HALF : (half + 1) * HALF, :] = value
        return value

    inner(table, every, wide, jac, picked, grad, spread, rest, loads[1:])


def inner_second(table, every, wide, jac, grad, volume, rest, picked):
    def here(half):
        return volume[half * HALF : (half + 1) * HALF, :]

    inner(table, every, wide, jac, picked, grad, here, rest, ())


def finish_kernel(last, *refs):
    rest, came, above, below, wide, jac, dinv, live = refs[:8]
    if last:
        out, halos = refs[8:]
    else:
        rows, swap, own, copies, table, halos = refs[8:]
    first = (lax.axis_index("dom") & 1) == 0
    for var in range(NV):
        halos[0, var] = jnp.where(first, above[1, var], came[0, var])
        halos[1, var] = jnp.where(first, came[1, var], below[1, var])
        halos[2, var] = above[0, var]
        halos[3, var] = below[0, var]
    for half in range(2):
        here = slice(half * HALF, (half + 1) * HALF)
        left = [rest[i, here, :] for i in range(NV)]
        for k in range(NEAR, NBR):
            lane, masks = split(wide[k, here, :] - BLOCKS * LANES, SLOTS)
            for var in range(NV):
                got = pick_lanes(halos[0, var], lane)
                for slot in range(1, SLOTS):
                    got = jnp.where(masks[slot], pick_lanes(halos[slot, var], lane), got)
                for i in range(NV):
                    left[i] = left[i] - jac[k, i, var, here, :] * got
        for i in range(NV):
            total = dinv[i, 0, here, :] * left[0]
            for var in range(1, NV):
                total = total + dinv[i, var, here, :] * left[var]
            total = live[here, :] * total
            if last:
                out[i, here, :] = total
            else:
                fill_table(half, total, i, table)
                at = i * ROWS + half * HALF
                for peer in range(8):
                    copies[peer, at : at + HALF, :] = total
    if not last:
        send_blocks(table, rows[...], swap, own)


VMEM = pl.BlockSpec(memory_space=pltpu.VMEM)
HBM = pl.BlockSpec(memory_space=pltpu.HBM)
SMEM = pl.BlockSpec(memory_space=pltpu.SMEM)
COST = pl.CostEstimate(flops=1_000_000, bytes_accessed=4_000_000, transcendentals=0)
PARAMS = pltpu.CompilerParams(vmem_limit_bytes=8 * 1024 * 1024)


def f32(*shape):
    return jax.ShapeDtypeStruct(shape, jnp.float32)


def i32(*shape):
    return jax.ShapeDtypeStruct(shape, jnp.int32)


TABLE = f32(NV, BLOCKS, HALF, LANES)
PAIR = f32(2, NV, HALF, LANES)
CURRENT = f32(NV, ROWS, LANES)
COPIES = f32(8, NV * ROWS, LANES)
WIDE = i32(NBR, ROWS, LANES)
ROW_INDEX = i32(HALF, LANES)
JAC = f32(NBR, NV, NV, ROWS, LANES)
DINV = f32(NV, NV, ROWS, LANES)
CELL = f32(ROWS, LANES)
PICKED = pltpu.VMEM((NEAR, NV, ROWS, LANES), jnp.float32)
HALOS = pltpu.VMEM((SLOTS, NV, HALF, LANES), jnp.float32)


def call(kernel, name, args, outs, scratch=(), hbm=(), smem=(), cost=None):
    specs = [HBM if n in hbm else SMEM if n in smem else VMEM for n in range(len(args))]
    args = [
        pltpu.with_memory_space_constraint(arg, pltpu.HBM) if n in hbm else arg
        for n, arg in enumerate(args)
    ]
    return pl.pallas_call(
        kernel,
        out_shape=outs,
        in_specs=specs,
        out_specs=jax.tree.map(lambda _: VMEM, outs),
        scratch_shapes=scratch,
        compiler_params=PARAMS,
        cost_estimate=cost,
        name=name,
    )(*args)


def swapped(value):
    count = lax.axis_size("dom")
    return lax.ppermute(value, "dom", [(source, source ^ 1) for source in range(count)])


def shifted(value, steps):
    count = lax.axis_size("dom")
    pairs = [(source, (source + steps) % count) for source in range(count)]
    return lax.ppermute(value, "dom", pairs)


def on_device(adjoint, gradient, jac_blocks, diag_inverse, volume, columns, send_rows, counts):
    swap, own, copies, table, rows = call(
        prep_kernel,
        "prep",
        (dense(adjoint), send_rows),
        (PAIR, PAIR, COPIES, TABLE, ROW_INDEX),
        [
            pltpu.VMEM(CURRENT.shape, jnp.float32),
            pltpu.VMEM((SLOTS, LANES), jnp.int32),
            pltpu.SemaphoreType.DMA((2,)),
        ],
        hbm=(0, 1),
    )
    came = swapped(swap)
    every = lax.all_to_all(copies, "inst", 0, 0)
    plus, minus = call(join_kernel, "join_first", (own, came), (PAIR, PAIR))
    above, below = shifted(plus, 2), shifted(minus, -2)
    raw = (
        columns,
        dense(jac_blocks),
        dense(diag_inverse),
        dense(gradient),
        volume.reshape(BLOCKS, LANES),
        counts,
    )
    rest, wide, jac, dinv, grad, vol, live = call(
        inner_first,
        "inner_first",
        (table, every) + raw,
        (CURRENT, WIDE, JAC, DINV, CURRENT, CELL, CELL),
        [
            PICKED,
            pltpu.VMEM((NBR, BLOCKS * LANES), jnp.int32),
            pltpu.VMEM((BLOCKS, LANES), jnp.float32),
            pltpu.SemaphoreType.DMA((5,)),
        ],
        hbm=range(2, 7),
        smem=(7,),
        cost=COST,
    )
    swap, own, copies, table = call(
        functools.partial(finish_kernel, False),
        "finish_first",
        (rest, came, above, below, wide, jac, dinv, live, rows),
        (PAIR, PAIR, COPIES, TABLE),
        [HALOS],
    )
    came = swapped(swap)
    every = lax.all_to_all(copies, "inst", 0, 0)
    plus, minus = call(join_kernel, "join_second", (own, came), (PAIR, PAIR))
    above, below = shifted(plus, 2), shifted(minus, -2)
    rest = call(
        inner_second,
        "inner_second",
        (table, every, wide, jac, grad, vol),
        CURRENT,
        [PICKED],
        cost=COST,
    )
    out = call(
        functools.partial(finish_kernel, True),
        "finish_second",
        (rest, came, above, below, wide, jac, dinv, live),
        CURRENT,
        [HALOS],
    )
    return undense(out)


def solution(mesh):
    in_specs = (
        P("inst", None, "dom"),
        P("inst", None, "dom"),
        P("inst", None, None, None, "dom"),
        P("inst", None, None, "dom"),
        P("dom"),
        P(None, "dom"),
        P("dom", None),
        P("dom"),
    )
    out_specs = P("inst", None, "dom")
    return jax.shard_map(
        on_device, mesh=mesh, in_specs=in_specs, out_specs=out_specs, check_vma=False
    )
```

```python
import functools
import math

import jax
import jax.numpy as jnp
from jax import lax
from jax.experimental import pallas as pl
from jax.experimental.pallas import tpu as pltpu
from jax.sharding import PartitionSpec as P

NI = 16
NV = 5
NBR = 6
NEAR = 4
SLOTS = 4
LANES = 128
ROWS = 16
HALF = 8
BLOCKS = 8


def spectral(diff):
    diff = diff % NI
    if diff == 0:
        return 0.0
    angle = math.pi * diff / NI
    return 0.5 * (-1) ** diff * math.cos(angle) / math.sin(angle)


def dense(x):
    lead = x.shape[1:-1]
    n = len(lead)
    y = x.reshape((2,) + lead + (BLOCKS, LANES))
    y = y.transpose(tuple(range(1, n + 1)) + (n + 1, 0, n + 2))
    return y.reshape(lead + (ROWS, LANES))


def undense(y):
    lead = y.shape[:-2]
    n = len(lead)
    y = y.reshape(lead + (BLOCKS, 2, LANES))
    y = y.transpose((n + 1,) + tuple(range(n)) + (n, n + 2))
    return y.reshape((2,) + lead + (BLOCKS * LANES,))


def row_iota():
    return lax.broadcasted_iota(jnp.int32, (HALF, LANES), 0)


def pick_lanes(x, index):
    return jnp.take_along_axis(x, index, axis=1, mode="promise_in_bounds")


def pick_rows(x, index):
    return jnp.take_along_axis(x, index, axis=0, mode="promise_in_bounds")


def fill_table(half, value, var, table):
    parity = row_iota() & 1
    for q in range(4):
        table[var, 4 * half + q] = pick_rows(value, parity + 2 * q)


def pick(table, var, lane, masks):
    got = pick_lanes(table[var, 0], lane)
    for block in range(1, len(masks)):
        got = jnp.where(masks[block], pick_lanes(table[var, block], lane), got)
    return got


def split(index, blocks):
    high = lax.shift_right_logical(index, 7)
    return index & (LANES - 1), [high == block for block in range(blocks)]


def send_blocks(table, rows, swap, own):
    lane, masks = split(rows, BLOCKS)
    parity = row_iota() & 1
    for var in range(NV):
        got = pick(table, var, lane, masks)
        for slot in range(SLOTS):
            out = (swap, swap, own, own)[slot]
            out[slot % 2, var] = pick_rows(got, parity + 2 * slot)


def prep_kernel(adj_hbm, sends_hbm, swap, own, copies, table, rows, adj, sends, sems):
    loads = [
        pltpu.make_async_copy(adj_hbm, adj, sems.at[0]),
        pltpu.make_async_copy(sends_hbm, sends, sems.at[1]),
    ]
    repeats = [
        pltpu.make_async_copy(adj_hbm, copies.at[peer], sems.at[2 + peer]) for peer in range(8)
    ]
    for copy in loads + repeats:
        copy.start()
    for load in loads:
        load.wait()
    for var in range(NV):
        for half in range(2):
            fill_table(half, adj[var, half * HALF : (half + 1) * HALF, :], var, table)
    for slot in range(SLOTS):
        rows[2 * slot : 2 * slot + 2, :] = jnp.broadcast_to(sends[slot : slot + 1, :], (2, LANES))
    send_blocks(table, rows[...], swap, own)
    for copy in repeats:
        copy.wait()


def join_kernel(own, came, plus, minus):
    for var in range(NV):
        plus[0, var] = own[0, var]
        plus[1, var] = came[0, var]
        minus[0, var] = own[1, var]
        minus[1, var] = came[1, var]


def timewise(every, me, var, half):
    row = row_iota()
    odd = (row & 1) == 1
    here = slice(half * HALF, (half + 1) * HALF)
    same = jnp.zeros((HALF, LANES), jnp.float32)
    cross = jnp.zeros((HALF, LANES), jnp.float32)
    for r in range(8):
        value = every[lax.rem(me + r, 8), var, here, :]
        if r:
            same = same + spectral(2 * r) * value
        factor = jnp.where(odd, spectral(2 * r + 1), spectral(2 * r - 1))
        cross = cross + factor.astype(jnp.float32) * value
    return same + pick_rows(cross, row ^ 1)


def inner(table, every, wide, jac, picked, grad, volume, rest, loads):
    me = lax.axis_index("inst")
    for half in range(2):
        here = slice(half * HALF, (half + 1) * HALF)
        for k in range(NEAR):
            lane, masks = split(wide[k, here, :], BLOCKS)
            for var in range(NV):
                picked[k, var, here, :] = pick(table, var, lane, masks)
        for var in range(NV):
            rest[var, here, :] = timewise(every, me, var, half)
    for load in loads:
        load.wait()
    for half in range(2):
        here = slice(half * HALF, (half + 1) * HALF)
        total = [None] * NV
        for k in range(NEAR):
            for var in range(NV):
                got = picked[k, var, here, :]
                for i in range(NV):
                    term = jac[k, i, var, here, :] * got
                    total[i] = term if total[i] is None else total[i] + term
        for i in range(NV):
            rest[i, here, :] = grad[i, here, :] - total[i] - volume(half) * rest[i, here, :]


def inner_first(
    table, every, cols_hbm, jac_hbm, dinv_hbm, grad_hbm, vol_hbm, count,
    rest, wide, jac, dinv, grad, volume, live,
    picked, cols, vol, sems,
):
    pairs = (
        (cols_hbm, cols),
        (jac_hbm, jac),
        (vol_hbm, vol),
        (dinv_hbm, dinv),
        (grad_hbm, grad),
    )
    loads = [pltpu.make_async_copy(a, b, sems.at[n]) for n, (a, b) in enumerate(pairs)]
    for load in loads:
        load.start()
    row = row_iota()
    for half in range(2):
        cell = (lax.shift_right_logical(row, 1) + 4 * half) * LANES
        cell = cell + lax.broadcasted_iota(jnp.int32, (HALF, LANES), 1)
        live[half * HALF : (half + 1) * HALF, :] = (cell < count[0]).astype(jnp.float32)
    loads[0].wait()
    for k in range(NBR):
        for block in range(BLOCKS):
            one = cols[k : k + 1, block * LANES : (block + 1) * LANES]
            wide[k, 2 * block : 2 * block + 2, :] = jnp.broadcast_to(one, (2, LANES))

    def spread(half):
        value = pick_rows(vol[...], lax.shift_right_logical(row, 1) + 4 * half)
        volume[half * HALF : (half + 1) * HALF, :] = value
        return value

    inner(table, every, wide, jac, picked, grad, spread, rest, loads[1:])


def inner_second(table, every, wide, jac, grad, volume, rest, picked):
    def here(half):
        return volume[half * HALF : (half + 1) * HALF, :]

    inner(table, every, wide, jac, picked, grad, here, rest, ())


def finish_kernel(last, *refs):
    rest, came, above, below, wide, jac, dinv, live = refs[:8]
    if last:
        out, halos, fresh, sems = refs[8:]
    else:
        rows, swap, own, copies, table, halos, fresh, sems = refs[8:]
    writes = []
    first = (lax.axis_index("dom") & 1) == 0
    for var in range(NV):
        halos[0, var] = jnp.where(first, above[1, var], came[0, var])
        halos[1, var] = jnp.where(first, came[1, var], below[1, var])
        halos[2, var] = above[0, var]
        halos[3, var] = below[0, var]
    for half in range(2):
        here = slice(half * HALF, (half + 1) * HALF)
        left = [rest[i, here, :] for i in range(NV)]
        for k in range(NEAR, NBR):
            lane, masks = split(wide[k, here, :] - BLOCKS * LANES, SLOTS)
            for var in range(NV):
                got = pick_lanes(halos[0, var], lane)
                for slot in range(1, SLOTS):
                    got = jnp.where(masks[slot], pick_lanes(halos[slot, var], lane), got)
                for i in range(NV):
                    left[i] = left[i] - jac[k, i, var, here, :] * got
        for i in range(NV):
            total = dinv[i, 0, here, :] * left[0]
            for var in range(1, NV):
                total = total + dinv[i, var, here, :] * left[var]
            total = live[here, :] * total
            fresh[i, here, :] = total
            if not last:
                fill_table(half, total, i, table)
        if last:
            targets = [out]
        elif half == 1:
            targets = [copies.at[peer] for peer in range(8)]
        else:
            targets = []
        for target in targets:
            source = fresh
            if last:
                source, target = (ref.at[:, pl.ds(half * HALF, HALF), :] for ref in (fresh, target))
            writes.append(pltpu.make_async_copy(source, target, sems.at[len(writes)]))
            writes[-1].start()
    if not last:
        send_blocks(table, rows[...], swap, own)
    for write in writes:
        write.wait()


VMEM = pl.BlockSpec(memory_space=pltpu.VMEM)
HBM = pl.BlockSpec(memory_space=pltpu.HBM)
SMEM = pl.BlockSpec(memory_space=pltpu.SMEM)
COST = pl.CostEstimate(flops=1_000_000, bytes_accessed=4_000_000, transcendentals=0)
PARAMS = pltpu.CompilerParams(vmem_limit_bytes=8 * 1024 * 1024)


def f32(*shape):
    return jax.ShapeDtypeStruct(shape, jnp.float32)


def i32(*shape):
    return jax.ShapeDtypeStruct(shape, jnp.int32)


TABLE = f32(NV, BLOCKS, HALF, LANES)
PAIR = f32(2, NV, HALF, LANES)
CURRENT = f32(NV, ROWS, LANES)
COPIES = f32(8, NV, ROWS, LANES)
WIDE = i32(NBR, ROWS, LANES)
ROW_INDEX = i32(HALF, LANES)
JAC = f32(NBR, NV, NV, ROWS, LANES)
DINV = f32(NV, NV, ROWS, LANES)
CELL = f32(ROWS, LANES)
PICKED = pltpu.VMEM((NEAR, NV, ROWS, LANES), jnp.float32)
FRESH = pltpu.VMEM((NV, ROWS, LANES), jnp.float32)
HALOS = pltpu.VMEM((SLOTS, NV, HALF, LANES), jnp.float32)


def call(kernel, name, args, outs, scratch=(), hbm=(), smem=(), hbm_out=(), cost=None):
    specs = [HBM if n in hbm else SMEM if n in smem else VMEM for n in range(len(args))]
    args = [
        pltpu.with_memory_space_constraint(arg, pltpu.HBM) if n in hbm else arg
        for n, arg in enumerate(args)
    ]
    return pl.pallas_call(
        kernel,
        out_shape=outs,
        in_specs=specs,
        out_specs=jax.tree.map(lambda out: HBM if out in hbm_out else VMEM, outs),
        scratch_shapes=scratch,
        compiler_params=PARAMS,
        cost_estimate=cost,
        name=name,
    )(*args)


def swapped(value):
    count = lax.axis_size("dom")
    return lax.ppermute(value, "dom", [(source, source ^ 1) for source in range(count)])


def shifted(value, steps):
    count = lax.axis_size("dom")
    pairs = [(source, (source + steps) % count) for source in range(count)]
    return lax.ppermute(value, "dom", pairs)


def on_device(adjoint, gradient, jac_blocks, diag_inverse, volume, columns, send_rows, counts):
    swap, own, copies, table, rows = call(
        prep_kernel,
        "prep",
        (dense(adjoint), send_rows),
        (PAIR, PAIR, COPIES, TABLE, ROW_INDEX),
        [
            pltpu.VMEM(CURRENT.shape, jnp.float32),
            pltpu.VMEM((SLOTS, LANES), jnp.int32),
            pltpu.SemaphoreType.DMA((10,)),
        ],
        hbm=(0, 1),
        hbm_out=(COPIES,),
    )
    came = swapped(swap)
    every = lax.all_to_all(copies, "inst", 0, 0)
    plus, minus = call(join_kernel, "join_first", (own, came), (PAIR, PAIR))
    above, below = shifted(plus, 2), shifted(minus, -2)
    raw = (
        columns,
        dense(jac_blocks),
        dense(diag_inverse),
        dense(gradient),
        volume.reshape(BLOCKS, LANES),
        counts,
    )
    rest, wide, jac, dinv, grad, vol, live = call(
        inner_first,
        "inner_first",
        (table, every) + raw,
        (CURRENT, WIDE, JAC, DINV, CURRENT, CELL, CELL),
        [
            PICKED,
            pltpu.VMEM((NBR, BLOCKS * LANES), jnp.int32),
            pltpu.VMEM((BLOCKS, LANES), jnp.float32),
            pltpu.SemaphoreType.DMA((5,)),
        ],
        hbm=range(2, 7),
        smem=(7,),
        cost=COST,
    )
    swap, own, copies, table = call(
        functools.partial(finish_kernel, False),
        "finish_first",
        (rest, came, above, below, wide, jac, dinv, live, rows),
        (PAIR, PAIR, COPIES, TABLE),
        [HALOS, FRESH, pltpu.SemaphoreType.DMA((8,))],
        hbm_out=(COPIES,),
    )
    came = swapped(swap)
    every = lax.all_to_all(copies, "inst", 0, 0)
    plus, minus = call(join_kernel, "join_second", (own, came), (PAIR, PAIR))
    above, below = shifted(plus, 2), shifted(minus, -2)
    rest = call(
        inner_second,
        "inner_second",
        (table, every, wide, jac, grad, vol),
        CURRENT,
        [PICKED],
        cost=COST,
    )
    out = call(
        functools.partial(finish_kernel, True),
        "finish_second",
        (rest, came, above, below, wide, jac, dinv, live),
        CURRENT,
        [HALOS, FRESH, pltpu.SemaphoreType.DMA((2,))],
        hbm_out=(CURRENT,),
    )
    return undense(out)


def solution(mesh):
    in_specs = (
        P("inst", None, "dom"),
        P("inst", None, "dom"),
        P("inst", None, None, None, "dom"),
        P("inst", None, None, "dom"),
        P("dom"),
        P(None, "dom"),
        P("dom", None),
        P("dom"),
    )
    out_specs = P("inst", None, "dom")
    return jax.shard_map(
        on_device, mesh=mesh, in_specs=in_specs, out_specs=out_specs, check_vma=False
    )
```

```python
import functools
import math

import jax
import jax.numpy as jnp
from jax import lax
from jax.experimental import pallas as pl
from jax.experimental.pallas import tpu as pltpu
from jax.sharding import PartitionSpec as P

NI = 16
NV = 5
NBR = 6
NEAR = 4
SLOTS = 4
LANES = 128
ROWS = 16
HALF = 8
BLOCKS = 8


def spectral(diff):
    diff = diff % NI
    if diff == 0:
        return 0.0
    angle = math.pi * diff / NI
    return 0.5 * (-1) ** diff * math.cos(angle) / math.sin(angle)


def dense(x):
    lead = x.shape[1:-1]
    n = len(lead)
    y = x.reshape((2,) + lead + (BLOCKS, LANES))
    y = y.transpose(tuple(range(1, n + 1)) + (n + 1, 0, n + 2))
    return y.reshape(lead + (ROWS, LANES))


def undense(y):
    lead = y.shape[:-2]
    n = len(lead)
    y = y.reshape(lead + (BLOCKS, 2, LANES))
    y = y.transpose((n + 1,) + tuple(range(n)) + (n, n + 2))
    return y.reshape((2,) + lead + (BLOCKS * LANES,))


def row_iota():
    return lax.broadcasted_iota(jnp.int32, (HALF, LANES), 0)


def pick_lanes(x, index):
    return jnp.take_along_axis(x, index, axis=1, mode="promise_in_bounds")


def pick_rows(x, index):
    return jnp.take_along_axis(x, index, axis=0, mode="promise_in_bounds")


def fill_table(half, value, var, table):
    parity = row_iota() & 1
    for q in range(4):
        table[var, 4 * half + q] = pick_rows(value, parity + 2 * q)


def pick(table, var, lane, masks):
    got = pick_lanes(table[var, 0], lane)
    for block in range(1, len(masks)):
        got = jnp.where(masks[block], pick_lanes(table[var, block], lane), got)
    return got


def split(index, blocks):
    high = lax.shift_right_logical(index, 7)
    return index & (LANES - 1), [high == block for block in range(blocks)]


def send_blocks(table, rows, swap, own):
    lane, masks = split(rows, BLOCKS)
    parity = row_iota() & 1
    for var in range(NV):
        got = pick(table, var, lane, masks)
        for slot in range(SLOTS):
            out = (swap, swap, own, own)[slot]
            out[slot % 2, var] = pick_rows(got, parity + 2 * slot)


def prep_kernel(
    adj_hbm, sends_hbm, cols_hbm, jac_hbm, dinv_hbm, grad_hbm, vol_hbm,
    swap, own, copies, table, rows, cols, jac, dinv, grad, vol,
    adj, sends, sems,
):
    pairs = (
        (adj_hbm, adj),
        (sends_hbm, sends),
        (cols_hbm, cols),
        (jac_hbm, jac),
        (dinv_hbm, dinv),
        (grad_hbm, grad),
        (vol_hbm, vol),
    )
    loads = [pltpu.make_async_copy(a, b, sems.at[n]) for n, (a, b) in enumerate(pairs)]
    for load in loads:
        load.start()
    loads[0].wait()
    for var in range(NV):
        for half in range(2):
            value = adj[var, half * HALF : (half + 1) * HALF, :]
            fill_table(half, value, var, table)
            for peer in range(8):
                at = var * ROWS + half * HALF
                copies[peer, at : at + HALF, :] = value
    loads[1].wait()
    for slot in range(SLOTS):
        rows[2 * slot : 2 * slot + 2, :] = jnp.broadcast_to(sends[slot : slot + 1, :], (2, LANES))
    send_blocks(table, rows[...], swap, own)
    for load in loads[2:]:
        load.wait()


def join_kernel(own, came, _, plus, minus):
    for var in range(NV):
        plus[0, var] = own[0, var]
        plus[1, var] = came[0, var]
        minus[0, var] = own[1, var]
        minus[1, var] = came[1, var]


def near_sum(table, wide, jac, grad, rest):
    for half in range(2):
        here = slice(half * HALF, (half + 1) * HALF)
        left = [grad[i, here, :] for i in range(NV)]
        for k in range(NEAR):
            lane, masks = split(wide[k, here, :], BLOCKS)
            for var in range(NV):
                got = pick(table, var, lane, masks)
                for i in range(NV):
                    left[i] = left[i] - jac[k, i, var, here, :] * got
        for i in range(NV):
            rest[i, here, :] = left[i]


def near_first(table, cols, jac, grad, vol, count, rest, wide, volume, live):
    row = row_iota()
    for half in range(2):
        here = slice(half * HALF, (half + 1) * HALF)
        block = lax.shift_right_logical(row, 1) + 4 * half
        volume[here, :] = pick_rows(vol[...], block)
        cell = block * LANES + lax.broadcasted_iota(jnp.int32, (HALF, LANES), 1)
        live[here, :] = (cell < count[0]).astype(jnp.float32)
    for k in range(NBR):
        for block in range(BLOCKS):
            one = cols[k : k + 1, block * LANES : (block + 1) * LANES]
            wide[k, 2 * block : 2 * block + 2, :] = jnp.broadcast_to(one, (2, LANES))
    near_sum(table, wide, jac, grad, rest)


def near_second(table, wide, jac, grad, rest):
    near_sum(table, wide, jac, grad, rest)


def timewise(every, me, var, half):
    row = row_iota()
    odd = (row & 1) == 1
    at = var * ROWS + half * HALF
    same = jnp.zeros((HALF, LANES), jnp.float32)
    cross = jnp.zeros((HALF, LANES), jnp.float32)
    for r in range(8):
        value = every[lax.rem(me + r, 8), at : at + HALF, :]
        if r:
            same = same + spectral(2 * r) * value
        factor = jnp.where(odd, spectral(2 * r + 1), spectral(2 * r - 1))
        cross = cross + factor.astype(jnp.float32) * value
    return same + pick_rows(cross, row ^ 1)


def finish_kernel(last, *refs):
    every, rest, came, above, below, wide, jac, dinv, volume, live = refs[:10]
    if last:
        out, halos = refs[10:]
    else:
        rows, swap, own, copies, table, halos = refs[10:]
    me = lax.axis_index("inst")
    first = (lax.axis_index("dom") & 1) == 0
    for var in range(NV):
        halos[0, var] = jnp.where(first, above[1, var], came[0, var])
        halos[1, var] = jnp.where(first, came[1, var], below[1, var])
        halos[2, var] = above[0, var]
        halos[3, var] = below[0, var]
    for half in range(2):
        here = slice(half * HALF, (half + 1) * HALF)
        left = [
            rest[i, here, :] - volume[here, :] * timewise(every, me, i, half) for i in range(NV)
        ]
        for k in range(NEAR, NBR):
            lane, masks = split(wide[k, here, :] - BLOCKS * LANES, SLOTS)
            for var in range(NV):
                got = pick_lanes(halos[0, var], lane)
                for slot in range(1, SLOTS):
                    got = jnp.where(masks[slot], pick_lanes(halos[slot, var], lane), got)
                for i in range(NV):
                    left[i] = left[i] - jac[k, i, var, here, :] * got
        for i in range(NV):
            total = dinv[i, 0, here, :] * left[0]
            for var in range(1, NV):
                total = total + dinv[i, var, here, :] * left[var]
            total = live[here, :] * total
            if last:
                out[i, here, :] = total
            else:
                fill_table(half, total, i, table)
                at = i * ROWS + half * HALF
                for peer in range(8):
                    copies[peer, at : at + HALF, :] = total
    if not last:
        send_blocks(table, rows[...], swap, own)


VMEM = pl.BlockSpec(memory_space=pltpu.VMEM)
HBM = pl.BlockSpec(memory_space=pltpu.HBM)
SMEM = pl.BlockSpec(memory_space=pltpu.SMEM)
COST = pl.CostEstimate(flops=1_000_000, bytes_accessed=4_000_000, transcendentals=0)
PARAMS = pltpu.CompilerParams(vmem_limit_bytes=8 * 1024 * 1024)


def f32(*shape):
    return jax.ShapeDtypeStruct(shape, jnp.float32)


def i32(*shape):
    return jax.ShapeDtypeStruct(shape, jnp.int32)


TABLE = f32(NV, BLOCKS, HALF, LANES)
PAIR = f32(2, NV, HALF, LANES)
CURRENT = f32(NV, ROWS, LANES)
COPIES = f32(8, NV * ROWS, LANES)
WIDE = i32(NBR, ROWS, LANES)
ROW_INDEX = i32(HALF, LANES)
JAC = f32(NBR, NV, NV, ROWS, LANES)
DINV = f32(NV, NV, ROWS, LANES)
CELL = f32(ROWS, LANES)
COLS = i32(NBR, BLOCKS * LANES)
VOL = f32(BLOCKS, LANES)
HALOS = pltpu.VMEM((SLOTS, NV, HALF, LANES), jnp.float32)


def call(kernel, name, args, outs, scratch=(), hbm=(), smem=(), cost=None):
    specs = [HBM if n in hbm else SMEM if n in smem else VMEM for n in range(len(args))]
    args = [
        pltpu.with_memory_space_constraint(arg, pltpu.HBM) if n in hbm else arg
        for n, arg in enumerate(args)
    ]
    return pl.pallas_call(
        kernel,
        out_shape=outs,
        in_specs=specs,
        out_specs=jax.tree.map(lambda _: VMEM, outs),
        scratch_shapes=scratch,
        compiler_params=PARAMS,
        cost_estimate=cost,
        name=name,
    )(*args)


def swapped(value):
    count = lax.axis_size("dom")
    return lax.ppermute(value, "dom", [(source, source ^ 1) for source in range(count)])


def shifted(value, steps):
    count = lax.axis_size("dom")
    pairs = [(source, (source + steps) % count) for source in range(count)]
    return lax.ppermute(value, "dom", pairs)


def on_device(adjoint, gradient, jac_blocks, diag_inverse, volume, columns, send_rows, counts):
    swap, own, copies, table, rows, cols, jac, dinv, grad, vol = call(
        prep_kernel,
        "prep",
        (
            dense(adjoint),
            send_rows,
            columns,
            dense(jac_blocks),
            dense(diag_inverse),
            dense(gradient),
            volume.reshape(BLOCKS, LANES),
        ),
        (PAIR, PAIR, COPIES, TABLE, ROW_INDEX, COLS, JAC, DINV, CURRENT, VOL),
        [
            pltpu.VMEM(CURRENT.shape, jnp.float32),
            pltpu.VMEM((SLOTS, LANES), jnp.int32),
            pltpu.SemaphoreType.DMA((7,)),
        ],
        hbm=range(7),
    )
    came = swapped(swap)
    every = lax.all_to_all(copies, "inst", 0, 0)
    rest, wide, vol, live = call(
        near_first,
        "near_first",
        (table, cols, jac, grad, vol, counts),
        (CURRENT, WIDE, CELL, CELL),
        smem=(5,),
        cost=COST,
    )
    plus, minus = call(join_kernel, "join_first", (own, came, rest), (PAIR, PAIR))
    above, below = shifted(plus, 2), shifted(minus, -2)
    kept = (wide, jac, dinv, vol, live)
    swap, own, copies, table = call(
        functools.partial(finish_kernel, False),
        "finish_first",
        (every, rest, came, above, below) + kept + (rows,),
        (PAIR, PAIR, COPIES, TABLE),
        [HALOS],
    )
    came = swapped(swap)
    every = lax.all_to_all(copies, "inst", 0, 0)
    rest = call(near_second, "near_second", (table, wide, jac, grad), CURRENT, cost=COST)
    plus, minus = call(join_kernel, "join_second", (own, came, rest), (PAIR, PAIR))
    above, below = shifted(plus, 2), shifted(minus, -2)
    out = call(
        functools.partial(finish_kernel, True),
        "finish_second",
        (every, rest, came, above, below) + kept,
        CURRENT,
        [HALOS],
    )
    return undense(out)


def solution(mesh):
    in_specs = (
        P("inst", None, "dom"),
        P("inst", None, "dom"),
        P("inst", None, None, None, "dom"),
        P("inst", None, None, "dom"),
        P("dom"),
        P(None, "dom"),
        P("dom", None),
        P("dom"),
    )
    out_specs = P("inst", None, "dom")
    return jax.shard_map(
        on_device, mesh=mesh, in_specs=in_specs, out_specs=out_specs, check_vma=False
    )
```

```python
import functools
import math

import jax
import jax.numpy as jnp
from jax import lax
from jax.experimental import pallas as pl
from jax.experimental.pallas import tpu as pltpu
from jax.sharding import PartitionSpec as P

NI = 16
NV = 5
NBR = 6
NEAR = 4
SLOTS = 4
LANES = 128
ROWS = 16
HALF = 8
BLOCKS = 8


def spectral(diff):
    diff = diff % NI
    if diff == 0:
        return 0.0
    angle = math.pi * diff / NI
    return 0.5 * (-1) ** diff * math.cos(angle) / math.sin(angle)


def dense(x):
    lead = x.shape[1:-1]
    n = len(lead)
    y = x.reshape((2,) + lead + (BLOCKS, LANES))
    y = y.transpose(tuple(range(1, n + 1)) + (n + 1, 0, n + 2))
    return y.reshape(lead + (ROWS, LANES))


def undense(y):
    lead = y.shape[:-2]
    n = len(lead)
    y = y.reshape(lead + (BLOCKS, 2, LANES))
    y = y.transpose((n + 1,) + tuple(range(n)) + (n, n + 2))
    return y.reshape((2,) + lead + (BLOCKS * LANES,))


def row_iota():
    return lax.broadcasted_iota(jnp.int32, (HALF, LANES), 0)


def pick_lanes(x, index):
    return jnp.take_along_axis(x, index, axis=1, mode="promise_in_bounds")


def pick_rows(x, index):
    return jnp.take_along_axis(x, index, axis=0, mode="promise_in_bounds")


def fill_table(half, value, var, table):
    parity = row_iota() & 1
    for q in range(4):
        table[var, 4 * half + q] = pick_rows(value, parity + 2 * q)


def pick(table, var, lane, masks):
    got = pick_lanes(table[var, 0], lane)
    for block in range(1, len(masks)):
        got = jnp.where(masks[block], pick_lanes(table[var, block], lane), got)
    return got


def split(index, blocks):
    high = lax.shift_right_logical(index, 7)
    return index & (LANES - 1), [high == block for block in range(blocks)]


def send_blocks(table, rows, swap, own):
    lane, masks = split(rows, BLOCKS)
    parity = row_iota() & 1
    for var in range(NV):
        got = pick(table, var, lane, masks)
        for slot in range(SLOTS):
            out = (swap, swap, own, own)[slot]
            out[slot % 2, var] = pick_rows(got, parity + 2 * slot)


def prep_kernel(
    adj_hbm, sends_hbm, cols_hbm, jac_hbm, grad_hbm, vol_hbm,
    swap, own, copies, table, rows, cols, jac, grad, vol,
    adj, sends, sems,
):
    pairs = (
        (adj_hbm, adj),
        (sends_hbm, sends),
        (cols_hbm, cols),
        (jac_hbm.at[0:2], jac),
        (grad_hbm, grad),
        (vol_hbm, vol),
    )
    loads = [pltpu.make_async_copy(a, b, sems.at[n]) for n, (a, b) in enumerate(pairs)]
    for load in loads:
        load.start()
    loads[0].wait()
    for var in range(NV):
        for half in range(2):
            value = adj[var, half * HALF : (half + 1) * HALF, :]
            fill_table(half, value, var, table)
            for peer in range(8):
                at = var * ROWS + half * HALF
                copies[peer, at : at + HALF, :] = value
    loads[1].wait()
    for slot in range(SLOTS):
        rows[2 * slot : 2 * slot + 2, :] = jnp.broadcast_to(sends[slot : slot + 1, :], (2, LANES))
    send_blocks(table, rows[...], swap, own)
    for load in loads[2:]:
        load.wait()


def join_kernel(own, came, _, plus, minus):
    for var in range(NV):
        plus[0, var] = own[0, var]
        plus[1, var] = came[0, var]
        minus[0, var] = own[1, var]
        minus[1, var] = came[1, var]


def near_sum(table, wide, jac, start, before, rest):
    for half in range(2):
        here = slice(half * HALF, (half + 1) * HALF)
        left = [before[i, here, :] for i in range(NV)]
        for k in range(2):
            lane, masks = split(wide[start + k, here, :], BLOCKS)
            for var in range(NV):
                got = pick(table, var, lane, masks)
                for i in range(NV):
                    left[i] = left[i] - jac[k, i, var, here, :] * got
        for i in range(NV):
            rest[i, here, :] = left[i]


def near_first(
    table, cols, jac, jac_hbm, grad, vol, count, rest, wide, jac_two, volume, live, sem
):
    load = pltpu.make_async_copy(jac_hbm.at[2:4], jac_two, sem.at[0])
    load.start()
    row = row_iota()
    for half in range(2):
        here = slice(half * HALF, (half + 1) * HALF)
        block = lax.shift_right_logical(row, 1) + 4 * half
        volume[here, :] = pick_rows(vol[...], block)
        cell = block * LANES + lax.broadcasted_iota(jnp.int32, (HALF, LANES), 1)
        live[here, :] = (cell < count[0]).astype(jnp.float32)
    for k in range(NBR):
        for block in range(BLOCKS):
            one = cols[k : k + 1, block * LANES : (block + 1) * LANES]
            wide[k, 2 * block : 2 * block + 2, :] = jnp.broadcast_to(one, (2, LANES))
    near_sum(table, wide, jac, 0, grad, rest)
    load.wait()
    near_sum(table, wide, jac_two, 2, rest, rest)


def near_second(table, wide, jac, jac_two, grad, rest):
    near_sum(table, wide, jac, 0, grad, rest)
    near_sum(table, wide, jac_two, 2, rest, rest)


def load_kernel(_, jac_hbm, dinv_hbm, jac, dinv, sems):
    loads = [
        pltpu.make_async_copy(jac_hbm.at[4:6], jac, sems.at[0]),
        pltpu.make_async_copy(dinv_hbm, dinv, sems.at[1]),
    ]
    for load in loads:
        load.start()
    for load in loads:
        load.wait()


def timewise(every, me, var, half):
    row = row_iota()
    odd = (row & 1) == 1
    at = var * ROWS + half * HALF
    same = jnp.zeros((HALF, LANES), jnp.float32)
    cross = jnp.zeros((HALF, LANES), jnp.float32)
    for r in range(8):
        value = every[lax.rem(me + r, 8), at : at + HALF, :]
        if r:
            same = same + spectral(2 * r) * value
        factor = jnp.where(odd, spectral(2 * r + 1), spectral(2 * r - 1))
        cross = cross + factor.astype(jnp.float32) * value
    return same + pick_rows(cross, row ^ 1)


def finish_kernel(last, *refs):
    every, rest, came, above, below, wide, jac, dinv, volume, live = refs[:10]
    if last:
        out, halos = refs[10:]
    else:
        rows, swap, own, copies, table, halos = refs[10:]
    me = lax.axis_index("inst")
    first = (lax.axis_index("dom") & 1) == 0
    for var in range(NV):
        halos[0, var] = jnp.where(first, above[1, var], came[0, var])
        halos[1, var] = jnp.where(first, came[1, var], below[1, var])
        halos[2, var] = above[0, var]
        halos[3, var] = below[0, var]
    for half in range(2):
        here = slice(half * HALF, (half + 1) * HALF)
        left = [
            rest[i, here, :] - volume[here, :] * timewise(every, me, i, half) for i in range(NV)
        ]
        for k in range(NEAR, NBR):
            lane, masks = split(wide[k, here, :] - BLOCKS * LANES, SLOTS)
            for var in range(NV):
                got = pick_lanes(halos[0, var], lane)
                for slot in range(1, SLOTS):
                    got = jnp.where(masks[slot], pick_lanes(halos[slot, var], lane), got)
                for i in range(NV):
                    left[i] = left[i] - jac[k - NEAR, i, var, here, :] * got
        for i in range(NV):
            total = dinv[i, 0, here, :] * left[0]
            for var in range(1, NV):
                total = total + dinv[i, var, here, :] * left[var]
            total = live[here, :] * total
            if last:
                out[i, here, :] = total
            else:
                fill_table(half, total, i, table)
                at = i * ROWS + half * HALF
                for peer in range(8):
                    copies[peer, at : at + HALF, :] = total
    if not last:
        send_blocks(table, rows[...], swap, own)


VMEM = pl.BlockSpec(memory_space=pltpu.VMEM)
HBM = pl.BlockSpec(memory_space=pltpu.HBM)
SMEM = pl.BlockSpec(memory_space=pltpu.SMEM)
COST = pl.CostEstimate(flops=1_000_000, bytes_accessed=4_000_000, transcendentals=0)
PARAMS = pltpu.CompilerParams(vmem_limit_bytes=8 * 1024 * 1024)


def f32(*shape):
    return jax.ShapeDtypeStruct(shape, jnp.float32)


def i32(*shape):
    return jax.ShapeDtypeStruct(shape, jnp.int32)


TABLE = f32(NV, BLOCKS, HALF, LANES)
PAIR = f32(2, NV, HALF, LANES)
CURRENT = f32(NV, ROWS, LANES)
COPIES = f32(8, NV * ROWS, LANES)
WIDE = i32(NBR, ROWS, LANES)
ROW_INDEX = i32(HALF, LANES)
JAC = f32(2, NV, NV, ROWS, LANES)
DINV = f32(NV, NV, ROWS, LANES)
CELL = f32(ROWS, LANES)
COLS = i32(NBR, BLOCKS * LANES)
VOL = f32(BLOCKS, LANES)
HALOS = pltpu.VMEM((SLOTS, NV, HALF, LANES), jnp.float32)


def call(kernel, name, args, outs, scratch=(), hbm=(), smem=(), cost=None):
    specs = [HBM if n in hbm else SMEM if n in smem else VMEM for n in range(len(args))]
    args = [
        pltpu.with_memory_space_constraint(arg, pltpu.HBM) if n in hbm else arg
        for n, arg in enumerate(args)
    ]
    return pl.pallas_call(
        kernel,
        out_shape=outs,
        in_specs=specs,
        out_specs=jax.tree.map(lambda _: VMEM, outs),
        scratch_shapes=scratch,
        compiler_params=PARAMS,
        cost_estimate=cost,
        name=name,
    )(*args)


def swapped(value):
    count = lax.axis_size("dom")
    return lax.ppermute(value, "dom", [(source, source ^ 1) for source in range(count)])


def shifted(value, steps):
    count = lax.axis_size("dom")
    pairs = [(source, (source + steps) % count) for source in range(count)]
    return lax.ppermute(value, "dom", pairs)


def on_device(adjoint, gradient, jac_blocks, diag_inverse, volume, columns, send_rows, counts):
    jac_hbm = dense(jac_blocks)
    swap, own, copies, table, rows, cols, jac, grad, vol = call(
        prep_kernel,
        "prep",
        (
            dense(adjoint),
            send_rows,
            columns,
            jac_hbm,
            dense(gradient),
            volume.reshape(BLOCKS, LANES),
        ),
        (PAIR, PAIR, COPIES, TABLE, ROW_INDEX, COLS, JAC, CURRENT, VOL),
        [
            pltpu.VMEM(CURRENT.shape, jnp.float32),
            pltpu.VMEM((SLOTS, LANES), jnp.int32),
            pltpu.SemaphoreType.DMA((6,)),
        ],
        hbm=range(6),
    )
    came = swapped(swap)
    every = lax.all_to_all(copies, "inst", 0, 0)
    rest, wide, jac_two, vol, live = call(
        near_first,
        "near_first",
        (table, cols, jac, jac_hbm, grad, vol, counts),
        (CURRENT, WIDE, JAC, CELL, CELL),
        [pltpu.SemaphoreType.DMA((1,))],
        hbm=(3,),
        smem=(6,),
        cost=COST,
    )
    plus, minus = call(join_kernel, "join_first", (own, came, rest), (PAIR, PAIR))
    above, below = shifted(plus, 2), shifted(minus, -2)
    far, dinv = call(
        load_kernel,
        "load_rest",
        (plus, jac_hbm, dense(diag_inverse)),
        (JAC, DINV),
        [pltpu.SemaphoreType.DMA((2,))],
        hbm=(1, 2),
        cost=COST,
    )
    kept = (wide, far, dinv, vol, live)
    swap, own, copies, table = call(
        functools.partial(finish_kernel, False),
        "finish_first",
        (every, rest, came, above, below) + kept + (rows,),
        (PAIR, PAIR, COPIES, TABLE),
        [HALOS],
    )
    came = swapped(swap)
    every = lax.all_to_all(copies, "inst", 0, 0)
    rest = call(near_second, "near_second", (table, wide, jac, jac_two, grad), CURRENT, cost=COST)
    plus, minus = call(join_kernel, "join_second", (own, came, rest), (PAIR, PAIR))
    above, below = shifted(plus, 2), shifted(minus, -2)
    out = call(
        functools.partial(finish_kernel, True),
        "finish_second",
        (every, rest, came, above, below) + kept,
        CURRENT,
        [HALOS],
    )
    return undense(out)


def solution(mesh):
    in_specs = (
        P("inst", None, "dom"),
        P("inst", None, "dom"),
        P("inst", None, None, None, "dom"),
        P("inst", None, None, "dom"),
        P("dom"),
        P(None, "dom"),
        P("dom", None),
        P("dom"),
    )
    out_specs = P("inst", None, "dom")
    return jax.shard_map(
        on_device, mesh=mesh, in_specs=in_specs, out_specs=out_specs, check_vma=False
    )
```

```python
import functools
import math

import jax
import jax.numpy as jnp
from jax import lax
from jax.experimental import pallas as pl
from jax.experimental.pallas import tpu as pltpu
from jax.sharding import PartitionSpec as P

NI = 16
NV = 5
NBR = 6
NEAR = 4
SLOTS = 4
LANES = 128
ROWS = 16
HALF = 8
BLOCKS = 8


def spectral(diff):
    diff = diff % NI
    if diff == 0:
        return 0.0
    angle = math.pi * diff / NI
    return 0.5 * (-1) ** diff * math.cos(angle) / math.sin(angle)


def dense(x):
    lead = x.shape[1:-1]
    n = len(lead)
    y = x.reshape((2,) + lead + (BLOCKS, LANES))
    y = y.transpose(tuple(range(1, n + 1)) + (n + 1, 0, n + 2))
    return y.reshape(lead + (ROWS, LANES))


def undense(y):
    lead = y.shape[:-2]
    n = len(lead)
    y = y.reshape(lead + (BLOCKS, 2, LANES))
    y = y.transpose((n + 1,) + tuple(range(n)) + (n, n + 2))
    return y.reshape((2,) + lead + (BLOCKS * LANES,))


def row_iota():
    return lax.broadcasted_iota(jnp.int32, (HALF, LANES), 0)


def pick_lanes(x, index):
    return jnp.take_along_axis(x, index, axis=1, mode="promise_in_bounds")


def pick_rows(x, index):
    return jnp.take_along_axis(x, index, axis=0, mode="promise_in_bounds")


def fill_table(half, value, var, table):
    parity = row_iota() & 1
    for q in range(4):
        table[var, 4 * half + q] = pick_rows(value, parity + 2 * q)


def pick(table, var, lane, masks):
    got = pick_lanes(table[var, 0], lane)
    for block in range(1, len(masks)):
        got = jnp.where(masks[block], pick_lanes(table[var, block], lane), got)
    return got


def split(index, blocks):
    high = lax.shift_right_logical(index, 7)
    return index & (LANES - 1), [high == block for block in range(blocks)]


def send_blocks(table, rows, swap, own):
    lane, masks = split(rows, BLOCKS)
    parity = row_iota() & 1
    for var in range(NV):
        got = pick(table, var, lane, masks)
        for slot in range(SLOTS):
            out = (swap, swap, own, own)[slot]
            out[slot % 2, var] = pick_rows(got, parity + 2 * slot)


def prep_kernel(
    adj_hbm, sends_hbm, cols_hbm, jac_hbm, dinv_hbm, grad_hbm, vol_hbm,
    swap, own, copies, table, rows, cols, jac, dinv, grad, vol,
    adj, sends, sems,
):
    pairs = (
        (adj_hbm, adj),
        (sends_hbm, sends),
        (cols_hbm, cols),
        (jac_hbm, jac),
        (dinv_hbm, dinv),
        (grad_hbm, grad),
        (vol_hbm, vol),
    )
    loads = [pltpu.make_async_copy(a, b, sems.at[n]) for n, (a, b) in enumerate(pairs)]
    for load in loads:
        load.start()
    loads[0].wait()
    for var in range(NV):
        for half in range(2):
            value = adj[var, half * HALF : (half + 1) * HALF, :]
            fill_table(half, value, var, table)
            for peer in range(8):
                at = var * ROWS + half * HALF
                copies[peer, at : at + HALF, :] = value
    loads[1].wait()
    for slot in range(SLOTS):
        rows[2 * slot : 2 * slot + 2, :] = jnp.broadcast_to(sends[slot : slot + 1, :], (2, LANES))
    send_blocks(table, rows[...], swap, own)
    for load in loads[2:]:
        load.wait()


def even_chip():
    return (lax.axis_index("dom") & 2) == 0


def join_kernel(own, came, _, over_odd, over_even):
    even = even_chip()
    for var in range(NV):
        plus = own[0, var], came[0, var]
        minus = own[1, var], came[1, var]
        for n in range(2):
            over_odd[n, var] = jnp.where(even, minus[n], plus[n])
            over_even[n, var] = jnp.where(even, plus[n], minus[n])


def near_sum(table, wide, jac, grad, rest):
    for half in range(2):
        here = slice(half * HALF, (half + 1) * HALF)
        left = [grad[i, here, :] for i in range(NV)]
        for k in range(NEAR):
            lane, masks = split(wide[k, here, :], BLOCKS)
            for var in range(NV):
                got = pick(table, var, lane, masks)
                for i in range(NV):
                    left[i] = left[i] - jac[k, i, var, here, :] * got
        for i in range(NV):
            rest[i, here, :] = left[i]


def near_first(table, cols, jac, grad, vol, count, rest, wide, volume, live):
    row = row_iota()
    for half in range(2):
        here = slice(half * HALF, (half + 1) * HALF)
        block = lax.shift_right_logical(row, 1) + 4 * half
        volume[here, :] = pick_rows(vol[...], block)
        cell = block * LANES + lax.broadcasted_iota(jnp.int32, (HALF, LANES), 1)
        live[here, :] = (cell < count[0]).astype(jnp.float32)
    for k in range(NBR):
        for block in range(BLOCKS):
            one = cols[k : k + 1, block * LANES : (block + 1) * LANES]
            wide[k, 2 * block : 2 * block + 2, :] = jnp.broadcast_to(one, (2, LANES))
    near_sum(table, wide, jac, grad, rest)


def near_second(table, wide, jac, grad, rest):
    near_sum(table, wide, jac, grad, rest)


def timewise(every, me, var, half):
    row = row_iota()
    odd = (row & 1) == 1
    at = var * ROWS + half * HALF
    same = jnp.zeros((HALF, LANES), jnp.float32)
    cross = jnp.zeros((HALF, LANES), jnp.float32)
    for r in range(8):
        value = every[lax.rem(me + r, 8), at : at + HALF, :]
        if r:
            same = same + spectral(2 * r) * value
        factor = jnp.where(odd, spectral(2 * r + 1), spectral(2 * r - 1))
        cross = cross + factor.astype(jnp.float32) * value
    return same + pick_rows(cross, row ^ 1)


def finish_kernel(last, *refs):
    every, rest, came, over_odd, over_even, wide, jac, dinv, volume, live = refs[:10]
    if last:
        out, halos = refs[10:]
    else:
        rows, swap, own, copies, table, halos = refs[10:]
    me = lax.axis_index("inst")
    first = (lax.axis_index("dom") & 1) == 0
    even = even_chip()
    for var in range(NV):
        above = [jnp.where(even, over_odd[n, var], over_even[n, var]) for n in range(2)]
        below = [jnp.where(even, over_even[n, var], over_odd[n, var]) for n in range(2)]
        halos[0, var] = jnp.where(first, above[1], came[0, var])
        halos[1, var] = jnp.where(first, came[1, var], below[1])
        halos[2, var] = above[0]
        halos[3, var] = below[0]
    for half in range(2):
        here = slice(half * HALF, (half + 1) * HALF)
        left = [
            rest[i, here, :] - volume[here, :] * timewise(every, me, i, half) for i in range(NV)
        ]
        for k in range(NEAR, NBR):
            lane, masks = split(wide[k, here, :] - BLOCKS * LANES, SLOTS)
            for var in range(NV):
                got = pick_lanes(halos[0, var], lane)
                for slot in range(1, SLOTS):
                    got = jnp.where(masks[slot], pick_lanes(halos[slot, var], lane), got)
                for i in range(NV):
                    left[i] = left[i] - jac[k, i, var, here, :] * got
        for i in range(NV):
            total = dinv[i, 0, here, :] * left[0]
            for var in range(1, NV):
                total = total + dinv[i, var, here, :] * left[var]
            total = live[here, :] * total
            if last:
                out[i, here, :] = total
            else:
                fill_table(half, total, i, table)
                at = i * ROWS + half * HALF
                for peer in range(8):
                    copies[peer, at : at + HALF, :] = total
    if not last:
        send_blocks(table, rows[...], swap, own)


VMEM = pl.BlockSpec(memory_space=pltpu.VMEM)
HBM = pl.BlockSpec(memory_space=pltpu.HBM)
SMEM = pl.BlockSpec(memory_space=pltpu.SMEM)
COST = pl.CostEstimate(flops=1_000_000, bytes_accessed=4_000_000, transcendentals=0)
PARAMS = pltpu.CompilerParams(vmem_limit_bytes=8 * 1024 * 1024)


def f32(*shape):
    return jax.ShapeDtypeStruct(shape, jnp.float32)


def i32(*shape):
    return jax.ShapeDtypeStruct(shape, jnp.int32)


TABLE = f32(NV, BLOCKS, HALF, LANES)
PAIR = f32(2, NV, HALF, LANES)
CURRENT = f32(NV, ROWS, LANES)
COPIES = f32(8, NV * ROWS, LANES)
WIDE = i32(NBR, ROWS, LANES)
ROW_INDEX = i32(HALF, LANES)
JAC = f32(NBR, NV, NV, ROWS, LANES)
DINV = f32(NV, NV, ROWS, LANES)
CELL = f32(ROWS, LANES)
COLS = i32(NBR, BLOCKS * LANES)
VOL = f32(BLOCKS, LANES)
HALOS = pltpu.VMEM((SLOTS, NV, HALF, LANES), jnp.float32)


def call(kernel, name, args, outs, scratch=(), hbm=(), smem=(), cost=None):
    specs = [HBM if n in hbm else SMEM if n in smem else VMEM for n in range(len(args))]
    args = [
        pltpu.with_memory_space_constraint(arg, pltpu.HBM) if n in hbm else arg
        for n, arg in enumerate(args)
    ]
    return pl.pallas_call(
        kernel,
        out_shape=outs,
        in_specs=specs,
        out_specs=jax.tree.map(lambda _: VMEM, outs),
        scratch_shapes=scratch,
        compiler_params=PARAMS,
        cost_estimate=cost,
        name=name,
    )(*args)


def swapped(value):
    count = lax.axis_size("dom")
    return lax.ppermute(value, "dom", [(source, source ^ 1) for source in range(count)])


def edge(value, odd):
    count = lax.axis_size("dom")
    pairs = []
    for source in range(count):
        up = (source // 2) % 2 == odd
        pairs.append((source, (source + (2 if up else -2)) % count))
    return lax.ppermute(value, "dom", pairs)


def on_device(adjoint, gradient, jac_blocks, diag_inverse, volume, columns, send_rows, counts):
    swap, own, copies, table, rows, cols, jac, dinv, grad, vol = call(
        prep_kernel,
        "prep",
        (
            dense(adjoint),
            send_rows,
            columns,
            dense(jac_blocks),
            dense(diag_inverse),
            dense(gradient),
            volume.reshape(BLOCKS, LANES),
        ),
        (PAIR, PAIR, COPIES, TABLE, ROW_INDEX, COLS, JAC, DINV, CURRENT, VOL),
        [
            pltpu.VMEM(CURRENT.shape, jnp.float32),
            pltpu.VMEM((SLOTS, LANES), jnp.int32),
            pltpu.SemaphoreType.DMA((7,)),
        ],
        hbm=range(7),
    )
    came = swapped(swap)
    every = lax.all_to_all(copies, "inst", 0, 0)
    rest, wide, vol, live = call(
        near_first,
        "near_first",
        (table, cols, jac, grad, vol, counts),
        (CURRENT, WIDE, CELL, CELL),
        smem=(5,),
        cost=COST,
    )
    odd, even = call(join_kernel, "join_first", (own, came, rest), (PAIR, PAIR))
    odd, even = edge(odd, 1), edge(even, 0)
    kept = (wide, jac, dinv, vol, live)
    swap, own, copies, table = call(
        functools.partial(finish_kernel, False),
        "finish_first",
        (every, rest, came, odd, even) + kept + (rows,),
        (PAIR, PAIR, COPIES, TABLE),
        [HALOS],
    )
    came = swapped(swap)
    every = lax.all_to_all(copies, "inst", 0, 0)
    rest = call(near_second, "near_second", (table, wide, jac, grad), CURRENT, cost=COST)
    odd, even = call(join_kernel, "join_second", (own, came, rest), (PAIR, PAIR))
    odd, even = edge(odd, 1), edge(even, 0)
    out = call(
        functools.partial(finish_kernel, True),
        "finish_second",
        (every, rest, came, odd, even) + kept,
        CURRENT,
        [HALOS],
    )
    return undense(out)


def solution(mesh):
    in_specs = (
        P("inst", None, "dom"),
        P("inst", None, "dom"),
        P("inst", None, None, None, "dom"),
        P("inst", None, None, "dom"),
        P("dom"),
        P(None, "dom"),
        P("dom", None),
        P("dom"),
    )
    out_specs = P("inst", None, "dom")
    return jax.shard_map(
        on_device, mesh=mesh, in_specs=in_specs, out_specs=out_specs, check_vma=False
    )
```

```python
import functools
import math

import jax
import jax.numpy as jnp
from jax import lax
from jax.experimental import pallas as pl
from jax.experimental.pallas import tpu as pltpu
from jax.sharding import PartitionSpec as P

NI = 16
NV = 5
NBR = 6
NEAR = 4
SLOTS = 4
LANES = 128
ROWS = 16
HALF = 8
BLOCKS = 8


def spectral(diff):
    diff = diff % NI
    if diff == 0:
        return 0.0
    angle = math.pi * diff / NI
    return 0.5 * (-1) ** diff * math.cos(angle) / math.sin(angle)


def dense(x):
    lead = x.shape[1:-1]
    n = len(lead)
    y = x.reshape((2,) + lead + (BLOCKS, LANES))
    y = y.transpose(tuple(range(1, n + 1)) + (n + 1, 0, n + 2))
    return y.reshape(lead + (ROWS, LANES))


def undense(y):
    lead = y.shape[:-2]
    n = len(lead)
    y = y.reshape(lead + (BLOCKS, 2, LANES))
    y = y.transpose((n + 1,) + tuple(range(n)) + (n, n + 2))
    return y.reshape((2,) + lead + (BLOCKS * LANES,))


def row_iota():
    return lax.broadcasted_iota(jnp.int32, (HALF, LANES), 0)


def pick_lanes(x, index):
    return jnp.take_along_axis(x, index, axis=1, mode="promise_in_bounds")


def pick_rows(x, index):
    return jnp.take_along_axis(x, index, axis=0, mode="promise_in_bounds")


def fill_table(half, value, var, table):
    parity = row_iota() & 1
    for q in range(4):
        table[var, 4 * half + q] = pick_rows(value, parity + 2 * q)


def pick(table, var, lane, masks):
    got = pick_lanes(table[var, 0], lane)
    for block in range(1, len(masks)):
        got = jnp.where(masks[block], pick_lanes(table[var, block], lane), got)
    return got


def split(index, blocks):
    high = lax.shift_right_logical(index, 7)
    return index & (LANES - 1), [high == block for block in range(blocks)]


def send_blocks(table, rows, swap, own):
    lane, masks = split(rows, BLOCKS)
    parity = row_iota() & 1
    for var in range(NV):
        got = pick(table, var, lane, masks)
        for slot in range(SLOTS):
            out = (swap, swap, own, own)[slot]
            out[slot % 2, var] = pick_rows(got, parity + 2 * slot)


def prep_kernel(
    adj_hbm, sends_hbm, cols_hbm, jac_hbm, dinv_hbm, grad_hbm, vol_hbm,
    swap, own, copies, table, rows, cols, jac, dinv, grad, vol,
    adj, sends, sems,
):
    pairs = (
        (adj_hbm, adj),
        (sends_hbm, sends),
        (cols_hbm, cols),
        (jac_hbm, jac),
        (dinv_hbm, dinv),
        (grad_hbm, grad),
        (vol_hbm, vol),
    )
    loads = [pltpu.make_async_copy(a, b, sems.at[n]) for n, (a, b) in enumerate(pairs)]
    for load in loads:
        load.start()
    loads[0].wait()
    for var in range(NV):
        for half in range(2):
            value = adj[var, half * HALF : (half + 1) * HALF, :]
            fill_table(half, value, var, table)
            for peer in range(8):
                at = var * ROWS + half * HALF
                copies[peer, at : at + HALF, :] = value
    loads[1].wait()
    for slot in range(SLOTS):
        rows[2 * slot : 2 * slot + 2, :] = jnp.broadcast_to(sends[slot : slot + 1, :], (2, LANES))
    send_blocks(table, rows[...], swap, own)
    for load in loads[2:]:
        load.wait()


def even_chip():
    return (lax.axis_index("dom") & 2) == 0


def join_kernel(over_edges, own, came, _, one, two):
    even = even_chip()
    for var in range(NV):
        plus = own[0, var], came[0, var]
        minus = own[1, var], came[1, var]
        for n in range(2):
            one[n, var] = jnp.where(even, minus[n], plus[n]) if over_edges else plus[n]
            two[n, var] = jnp.where(even, plus[n], minus[n]) if over_edges else minus[n]


def near_sum(table, wide, jac, grad, rest):
    for half in range(2):
        here = slice(half * HALF, (half + 1) * HALF)
        left = [grad[i, here, :] for i in range(NV)]
        for k in range(NEAR):
            lane, masks = split(wide[k, here, :], BLOCKS)
            for var in range(NV):
                got = pick(table, var, lane, masks)
                for i in range(NV):
                    left[i] = left[i] - jac[k, i, var, here, :] * got
        for i in range(NV):
            rest[i, here, :] = left[i]


def near_first(table, cols, jac, grad, vol, count, rest, wide, volume, live):
    row = row_iota()
    for half in range(2):
        here = slice(half * HALF, (half + 1) * HALF)
        block = lax.shift_right_logical(row, 1) + 4 * half
        volume[here, :] = pick_rows(vol[...], block)
        cell = block * LANES + lax.broadcasted_iota(jnp.int32, (HALF, LANES), 1)
        live[here, :] = (cell < count[0]).astype(jnp.float32)
    for k in range(NBR):
        for block in range(BLOCKS):
            one = cols[k : k + 1, block * LANES : (block + 1) * LANES]
            wide[k, 2 * block : 2 * block + 2, :] = jnp.broadcast_to(one, (2, LANES))
    near_sum(table, wide, jac, grad, rest)


def near_second(table, wide, jac, grad, rest):
    near_sum(table, wide, jac, grad, rest)


def timewise(every, me, var, half):
    row = row_iota()
    odd = (row & 1) == 1
    at = var * ROWS + half * HALF
    same = jnp.zeros((HALF, LANES), jnp.float32)
    cross = jnp.zeros((HALF, LANES), jnp.float32)
    for r in range(8):
        value = every[lax.rem(me + r, 8), at : at + HALF, :]
        if r:
            same = same + spectral(2 * r) * value
        factor = jnp.where(odd, spectral(2 * r + 1), spectral(2 * r - 1))
        cross = cross + factor.astype(jnp.float32) * value
    return same + pick_rows(cross, row ^ 1)


def finish_kernel(last, *refs):
    every, rest, came, one, two, wide, jac, dinv, volume, live = refs[:10]
    if last:
        out, halos = refs[10:]
    else:
        rows, swap, own, copies, table, halos = refs[10:]
    me = lax.axis_index("inst")
    first = (lax.axis_index("dom") & 1) == 0
    even = even_chip()
    for var in range(NV):
        above = [one[n, var] for n in range(2)]
        below = [two[n, var] for n in range(2)]
        if last:
            above, below = (
                [jnp.where(even, a, b) for a, b in zip(above, below)],
                [jnp.where(even, b, a) for a, b in zip(above, below)],
            )
        halos[0, var] = jnp.where(first, above[1], came[0, var])
        halos[1, var] = jnp.where(first, came[1, var], below[1])
        halos[2, var] = above[0]
        halos[3, var] = below[0]
    for half in range(2):
        here = slice(half * HALF, (half + 1) * HALF)
        left = [
            rest[i, here, :] - volume[here, :] * timewise(every, me, i, half) for i in range(NV)
        ]
        for k in range(NEAR, NBR):
            lane, masks = split(wide[k, here, :] - BLOCKS * LANES, SLOTS)
            for var in range(NV):
                got = pick_lanes(halos[0, var], lane)
                for slot in range(1, SLOTS):
                    got = jnp.where(masks[slot], pick_lanes(halos[slot, var], lane), got)
                for i in range(NV):
                    left[i] = left[i] - jac[k, i, var, here, :] * got
        for i in range(NV):
            total = dinv[i, 0, here, :] * left[0]
            for var in range(1, NV):
                total = total + dinv[i, var, here, :] * left[var]
            total = live[here, :] * total
            if last:
                out[i, here, :] = total
            else:
                fill_table(half, total, i, table)
                at = i * ROWS + half * HALF
                for peer in range(8):
                    copies[peer, at : at + HALF, :] = total
    if not last:
        send_blocks(table, rows[...], swap, own)


VMEM = pl.BlockSpec(memory_space=pltpu.VMEM)
HBM = pl.BlockSpec(memory_space=pltpu.HBM)
SMEM = pl.BlockSpec(memory_space=pltpu.SMEM)
COST = pl.CostEstimate(flops=1_000_000, bytes_accessed=4_000_000, transcendentals=0)
PARAMS = pltpu.CompilerParams(vmem_limit_bytes=8 * 1024 * 1024)


def f32(*shape):
    return jax.ShapeDtypeStruct(shape, jnp.float32)


def i32(*shape):
    return jax.ShapeDtypeStruct(shape, jnp.int32)


TABLE = f32(NV, BLOCKS, HALF, LANES)
PAIR = f32(2, NV, HALF, LANES)
CURRENT = f32(NV, ROWS, LANES)
COPIES = f32(8, NV * ROWS, LANES)
WIDE = i32(NBR, ROWS, LANES)
ROW_INDEX = i32(HALF, LANES)
JAC = f32(NBR, NV, NV, ROWS, LANES)
DINV = f32(NV, NV, ROWS, LANES)
CELL = f32(ROWS, LANES)
COLS = i32(NBR, BLOCKS * LANES)
VOL = f32(BLOCKS, LANES)
HALOS = pltpu.VMEM((SLOTS, NV, HALF, LANES), jnp.float32)


def call(kernel, name, args, outs, scratch=(), hbm=(), smem=(), cost=None):
    specs = [HBM if n in hbm else SMEM if n in smem else VMEM for n in range(len(args))]
    args = [
        pltpu.with_memory_space_constraint(arg, pltpu.HBM) if n in hbm else arg
        for n, arg in enumerate(args)
    ]
    return pl.pallas_call(
        kernel,
        out_shape=outs,
        in_specs=specs,
        out_specs=jax.tree.map(lambda _: VMEM, outs),
        scratch_shapes=scratch,
        compiler_params=PARAMS,
        cost_estimate=cost,
        name=name,
    )(*args)


def swapped(value):
    count = lax.axis_size("dom")
    return lax.ppermute(value, "dom", [(source, source ^ 1) for source in range(count)])


def shifted(value, steps):
    count = lax.axis_size("dom")
    pairs = [(source, (source + steps) % count) for source in range(count)]
    return lax.ppermute(value, "dom", pairs)


def edge(value, odd):
    count = lax.axis_size("dom")
    pairs = []
    for source in range(count):
        up = (source // 2) % 2 == odd
        pairs.append((source, (source + (2 if up else -2)) % count))
    return lax.ppermute(value, "dom", pairs)


def on_device(adjoint, gradient, jac_blocks, diag_inverse, volume, columns, send_rows, counts):
    swap, own, copies, table, rows, cols, jac, dinv, grad, vol = call(
        prep_kernel,
        "prep",
        (
            dense(adjoint),
            send_rows,
            columns,
            dense(jac_blocks),
            dense(diag_inverse),
            dense(gradient),
            volume.reshape(BLOCKS, LANES),
        ),
        (PAIR, PAIR, COPIES, TABLE, ROW_INDEX, COLS, JAC, DINV, CURRENT, VOL),
        [
            pltpu.VMEM(CURRENT.shape, jnp.float32),
            pltpu.VMEM((SLOTS, LANES), jnp.int32),
            pltpu.SemaphoreType.DMA((7,)),
        ],
        hbm=range(7),
    )
    came = swapped(swap)
    every = lax.all_to_all(copies, "inst", 0, 0)
    rest, wide, vol, live = call(
        near_first,
        "near_first",
        (table, cols, jac, grad, vol, counts),
        (CURRENT, WIDE, CELL, CELL),
        smem=(5,),
        cost=COST,
    )
    plus, minus = call(
        functools.partial(join_kernel, False), "join_first", (own, came, rest), (PAIR, PAIR)
    )
    above, below = shifted(plus, 2), shifted(minus, -2)
    kept = (wide, jac, dinv, vol, live)
    swap, own, copies, table = call(
        functools.partial(finish_kernel, False),
        "finish_first",
        (every, rest, came, above, below) + kept + (rows,),
        (PAIR, PAIR, COPIES, TABLE),
        [HALOS],
    )
    came = swapped(swap)
    every = lax.all_to_all(copies, "inst", 0, 0)
    rest = call(near_second, "near_second", (table, wide, jac, grad), CURRENT, cost=COST)
    odd, even = call(
        functools.partial(join_kernel, True), "join_second", (own, came, rest), (PAIR, PAIR)
    )
    odd, even = edge(odd, 1), edge(even, 0)
    out = call(
        functools.partial(finish_kernel, True),
        "finish_second",
        (every, rest, came, odd, even) + kept,
        CURRENT,
        [HALOS],
    )
    return undense(out)


def solution(mesh):
    in_specs = (
        P("inst", None, "dom"),
        P("inst", None, "dom"),
        P("inst", None, None, None, "dom"),
        P("inst", None, None, "dom"),
        P("dom"),
        P(None, "dom"),
        P("dom", None),
        P("dom"),
    )
    out_specs = P("inst", None, "dom")
    return jax.shard_map(
        on_device, mesh=mesh, in_specs=in_specs, out_specs=out_specs, check_vma=False
    )
```

```python
import functools
import math

import jax
import jax.numpy as jnp
from jax import lax
from jax.experimental import pallas as pl
from jax.experimental.pallas import tpu as pltpu
from jax.sharding import PartitionSpec as P

NI = 16
NV = 5
NBR = 6
NEAR = 4
SLOTS = 4
LANES = 128
ROWS = 16
HALF = 8
BLOCKS = 8


def spectral(diff):
    diff = diff % NI
    if diff == 0:
        return 0.0
    angle = math.pi * diff / NI
    return 0.5 * (-1) ** diff * math.cos(angle) / math.sin(angle)


def dense(x):
    lead = x.shape[1:-1]
    n = len(lead)
    y = x.reshape((2,) + lead + (BLOCKS, LANES))
    y = y.transpose(tuple(range(1, n + 1)) + (n + 1, 0, n + 2))
    return y.reshape(lead + (ROWS, LANES))


def undense(y):
    lead = y.shape[:-2]
    n = len(lead)
    y = y.reshape(lead + (BLOCKS, 2, LANES))
    y = y.transpose((n + 1,) + tuple(range(n)) + (n, n + 2))
    return y.reshape((2,) + lead + (BLOCKS * LANES,))


def row_iota():
    return lax.broadcasted_iota(jnp.int32, (HALF, LANES), 0)


def pick_lanes(x, index):
    return jnp.take_along_axis(x, index, axis=1, mode="promise_in_bounds")


def pick_rows(x, index):
    return jnp.take_along_axis(x, index, axis=0, mode="promise_in_bounds")


def fill_table(half, value, var, table):
    parity = row_iota() & 1
    for q in range(4):
        table[var, 4 * half + q] = pick_rows(value, parity + 2 * q)


def pick(table, var, lane, masks):
    got = pick_lanes(table[var, 0], lane)
    for block in range(1, len(masks)):
        got = jnp.where(masks[block], pick_lanes(table[var, block], lane), got)
    return got


def split(index, blocks):
    high = lax.shift_right_logical(index, 7)
    return index & (LANES - 1), [high == block for block in range(blocks)]


def send_blocks(table, rows, swap, own):
    lane, masks = split(rows, BLOCKS)
    parity = row_iota() & 1
    for var in range(NV):
        got = pick(table, var, lane, masks)
        for slot in range(SLOTS):
            out = (swap, swap, own, own)[slot]
            out[slot % 2, var] = pick_rows(got, parity + 2 * slot)


def prep_kernel(adj_hbm, sends_hbm, swap, own, copies, table, rows, adj, sends, sems):
    loads = [
        pltpu.make_async_copy(adj_hbm, adj, sems.at[0]),
        pltpu.make_async_copy(sends_hbm, sends, sems.at[1]),
    ]
    for load in loads:
        load.start()
    loads[0].wait()
    repeats = [pltpu.make_async_copy(adj, copies.at[n], sems.at[2 + n]) for n in range(8)]
    for repeat in repeats:
        repeat.start()
    for var in range(NV):
        for half in range(2):
            at = var * ROWS + half * HALF
            fill_table(half, adj[at : at + HALF, :], var, table)
    loads[1].wait()
    for slot in range(SLOTS):
        rows[2 * slot : 2 * slot + 2, :] = jnp.broadcast_to(sends[slot : slot + 1, :], (2, LANES))
    send_blocks(table, rows[...], swap, own)
    for repeat in repeats:
        repeat.wait()


def join_kernel(own, came, plus, minus):
    for var in range(NV):
        plus[0, var] = own[0, var]
        plus[1, var] = came[0, var]
        minus[0, var] = own[1, var]
        minus[1, var] = came[1, var]


def timewise(every, me, var, half):
    row = row_iota()
    odd = (row & 1) == 1
    at = var * ROWS + half * HALF
    same = jnp.zeros((HALF, LANES), jnp.float32)
    cross = jnp.zeros((HALF, LANES), jnp.float32)
    for r in range(8):
        value = every[lax.rem(me + r, 8), at : at + HALF, :]
        if r:
            same = same + spectral(2 * r) * value
        factor = jnp.where(odd, spectral(2 * r + 1), spectral(2 * r - 1))
        cross = cross + factor.astype(jnp.float32) * value
    return same + pick_rows(cross, row ^ 1)


def inner(table, every, wide, jac, picked, grad, volume, rest, loads):
    me = lax.axis_index("inst")
    for half in range(2):
        here = slice(half * HALF, (half + 1) * HALF)
        for k in range(NEAR):
            lane, masks = split(wide[k, here, :], BLOCKS)
            for var in range(NV):
                picked[k, var, here, :] = pick(table, var, lane, masks)
        for var in range(NV):
            rest[var, here, :] = timewise(every, me, var, half)
    for load in loads:
        load.wait()
    for half in range(2):
        here = slice(half * HALF, (half + 1) * HALF)
        total = [None] * NV
        for k in range(NEAR):
            for var in range(NV):
                got = picked[k, var, here, :]
                for i in range(NV):
                    term = jac[k, i, var, here, :] * got
                    total[i] = term if total[i] is None else total[i] + term
        for i in range(NV):
            rest[i, here, :] = grad[i, here, :] - total[i] - volume(half) * rest[i, here, :]


def inner_first(
    table, every, cols_hbm, jac_hbm, dinv_hbm, grad_hbm, vol_hbm, count,
    rest, wide, jac, dinv, grad, volume, live,
    picked, cols, vol, sems,
):
    pairs = (
        (cols_hbm, cols),
        (jac_hbm, jac),
        (vol_hbm, vol),
        (dinv_hbm, dinv),
        (grad_hbm, grad),
    )
    loads = [pltpu.make_async_copy(a, b, sems.at[n]) for n, (a, b) in enumerate(pairs)]
    for load in loads:
        load.start()
    row = row_iota()
    for half in range(2):
        cell = (lax.shift_right_logical(row, 1) + 4 * half) * LANES
        cell = cell + lax.broadcasted_iota(jnp.int32, (HALF, LANES), 1)
        live[half * HALF : (half + 1) * HALF, :] = (cell < count[0]).astype(jnp.float32)
    loads[0].wait()
    for k in range(NBR):
        for block in range(BLOCKS):
            one = cols[k : k + 1, block * LANES : (block + 1) * LANES]
            wide[k, 2 * block : 2 * block + 2, :] = jnp.broadcast_to(one, (2, LANES))

    def spread(half):
        value = pick_rows(vol[...], lax.shift_right_logical(row, 1) + 4 * half)
        volume[half * HALF : (half + 1) * HALF, :] = value
        return value

    inner(table, every, wide, jac, picked, grad, spread, rest, loads[1:])


def inner_second(table, every, wide, jac, grad, volume, rest, picked):
    def here(half):
        return volume[half * HALF : (half + 1) * HALF, :]

    inner(table, every, wide, jac, picked, grad, here, rest, ())


def finish_kernel(last, *refs):
    rest, came, above, below, wide, jac, dinv, live = refs[:8]
    if last:
        out, halos = refs[8:]
    else:
        rows, swap, own, copies, table, halos = refs[8:]
    first = (lax.axis_index("dom") & 1) == 0
    for var in range(NV):
        halos[0, var] = jnp.where(first, above[1, var], came[0, var])
        halos[1, var] = jnp.where(first, came[1, var], below[1, var])
        halos[2, var] = above[0, var]
        halos[3, var] = below[0, var]
    for half in range(2):
        here = slice(half * HALF, (half + 1) * HALF)
        left = [rest[i, here, :] for i in range(NV)]
        for k in range(NEAR, NBR):
            lane, masks = split(wide[k, here, :] - BLOCKS * LANES, SLOTS)
            for var in range(NV):
                got = pick_lanes(halos[0, var], lane)
                for slot in range(1, SLOTS):
                    got = jnp.where(masks[slot], pick_lanes(halos[slot, var], lane), got)
                for i in range(NV):
                    left[i] = left[i] - jac[k, i, var, here, :] * got
        for i in range(NV):
            total = dinv[i, 0, here, :] * left[0]
            for var in range(1, NV):
                total = total + dinv[i, var, here, :] * left[var]
            total = live[here, :] * total
            if last:
                out[i, here, :] = total
            else:
                fill_table(half, total, i, table)
                at = i * ROWS + half * HALF
                for peer in range(8):
                    copies[peer, at : at + HALF, :] = total
    if not last:
        send_blocks(table, rows[...], swap, own)


VMEM = pl.BlockSpec(memory_space=pltpu.VMEM)
HBM = pl.BlockSpec(memory_space=pltpu.HBM)
SMEM = pl.BlockSpec(memory_space=pltpu.SMEM)
COST = pl.CostEstimate(flops=1_000_000, bytes_accessed=4_000_000, transcendentals=0)
PARAMS = pltpu.CompilerParams(vmem_limit_bytes=8 * 1024 * 1024)


def f32(*shape):
    return jax.ShapeDtypeStruct(shape, jnp.float32)


def i32(*shape):
    return jax.ShapeDtypeStruct(shape, jnp.int32)


TABLE = f32(NV, BLOCKS, HALF, LANES)
PAIR = f32(2, NV, HALF, LANES)
CURRENT = f32(NV, ROWS, LANES)
COPIES = f32(8, NV * ROWS, LANES)
WIDE = i32(NBR, ROWS, LANES)
ROW_INDEX = i32(HALF, LANES)
JAC = f32(NBR, NV, NV, ROWS, LANES)
DINV = f32(NV, NV, ROWS, LANES)
CELL = f32(ROWS, LANES)
PICKED = pltpu.VMEM((NEAR, NV, ROWS, LANES), jnp.float32)
HALOS = pltpu.VMEM((SLOTS, NV, HALF, LANES), jnp.float32)


def call(kernel, name, args, outs, scratch=(), hbm=(), smem=(), hbm_out=(), cost=None):
    specs = [HBM if n in hbm else SMEM if n in smem else VMEM for n in range(len(args))]
    args = [
        pltpu.with_memory_space_constraint(arg, pltpu.HBM) if n in hbm else arg
        for n, arg in enumerate(args)
    ]
    return pl.pallas_call(
        kernel,
        out_shape=outs,
        in_specs=specs,
        out_specs=jax.tree.map(lambda out: HBM if out in hbm_out else VMEM, outs),
        scratch_shapes=scratch,
        compiler_params=PARAMS,
        cost_estimate=cost,
        name=name,
    )(*args)


def swapped(value):
    count = lax.axis_size("dom")
    return lax.ppermute(value, "dom", [(source, source ^ 1) for source in range(count)])


def shifted(value, steps):
    count = lax.axis_size("dom")
    pairs = [(source, (source + steps) % count) for source in range(count)]
    return lax.ppermute(value, "dom", pairs)


def on_device(adjoint, gradient, jac_blocks, diag_inverse, volume, columns, send_rows, counts):
    swap, own, copies, table, rows = call(
        prep_kernel,
        "prep",
        (dense(adjoint).reshape(NV * ROWS, LANES), send_rows),
        (PAIR, PAIR, COPIES, TABLE, ROW_INDEX),
        [
            pltpu.VMEM((NV * ROWS, LANES), jnp.float32),
            pltpu.VMEM((SLOTS, LANES), jnp.int32),
            pltpu.SemaphoreType.DMA((10,)),
        ],
        hbm=(0, 1),
        hbm_out=(COPIES,),
    )
    came = swapped(swap)
    every = lax.all_to_all(copies, "inst", 0, 0)
    plus, minus = call(join_kernel, "join_first", (own, came), (PAIR, PAIR))
    above, below = shifted(plus, 2), shifted(minus, -2)
    raw = (
        columns,
        dense(jac_blocks),
        dense(diag_inverse),
        dense(gradient),
        volume.reshape(BLOCKS, LANES),
        counts,
    )
    rest, wide, jac, dinv, grad, vol, live = call(
        inner_first,
        "inner_first",
        (table, every) + raw,
        (CURRENT, WIDE, JAC, DINV, CURRENT, CELL, CELL),
        [
            PICKED,
            pltpu.VMEM((NBR, BLOCKS * LANES), jnp.int32),
            pltpu.VMEM((BLOCKS, LANES), jnp.float32),
            pltpu.SemaphoreType.DMA((5,)),
        ],
        hbm=range(2, 7),
        smem=(7,),
        cost=COST,
    )
    swap, own, copies, table = call(
        functools.partial(finish_kernel, False),
        "finish_first",
        (rest, came, above, below, wide, jac, dinv, live, rows),
        (PAIR, PAIR, COPIES, TABLE),
        [HALOS],
    )
    came = swapped(swap)
    every = lax.all_to_all(copies, "inst", 0, 0)
    plus, minus = call(join_kernel, "join_second", (own, came), (PAIR, PAIR))
    above, below = shifted(plus, 2), shifted(minus, -2)
    rest = call(
        inner_second,
        "inner_second",
        (table, every, wide, jac, grad, vol),
        CURRENT,
        [PICKED],
        cost=COST,
    )
    out = call(
        functools.partial(finish_kernel, True),
        "finish_second",
        (rest, came, above, below, wide, jac, dinv, live),
        CURRENT,
        [HALOS],
    )
    return undense(out)


def solution(mesh):
    in_specs = (
        P("inst", None, "dom"),
        P("inst", None, "dom"),
        P("inst", None, None, None, "dom"),
        P("inst", None, None, "dom"),
        P("dom"),
        P(None, "dom"),
        P("dom", None),
        P("dom"),
    )
    out_specs = P("inst", None, "dom")
    return jax.shard_map(
        on_device, mesh=mesh, in_specs=in_specs, out_specs=out_specs, check_vma=False
    )
```
